128 devices in a mesh: dp: 64 (over z, y, x), fsdp: 2 (over core).
Axes of the slice: x: 4, y: 4, z: 4, core: 2. Of those that a mesh axis runs over, the one named last changes fastest.
Arguments:
- tokens: bfloat16 [64, 157, 1408], P('dp', None, 'fsdp'), may hold values from -16 to 16
- vis_index: int32 [64, 157], P('dp'), may hold values from 0 to 1567, as said below
- owner: int32 [64, 1568], P('dp'), may hold values from 0 to 1, as said below
- enc_gain: bfloat16 [1408], replicated, may hold values from 0.5 to 1.5
- enc_qkv: bfloat16 [1408, 3, 1408], P(None, None, 'fsdp')
- enc_proj: bfloat16 [1408, 1408], P('fsdp'), may hold values from -0.15625 to 0.15625
- to_decoder: bfloat16 [1408, 512], replicated, may hold values from -0.15625 to 0.15625
- mask_token: bfloat16 [512], replicated, may hold values from -4 to 4
- dec_gain1: bfloat16 [512], replicated, may hold values from 0.5 to 1.5
- dec_qkv: bfloat16 [512, 768], replicated
- dec_proj: bfloat16 [256, 512], replicated, may hold values from -0.375 to 0.375
- dec_gain2: bfloat16 [512], replicated, may hold values from 0.5 to 1.5
- dec_fc1: bfloat16 [512, 2048], replicated, may hold values from -0.25 to 0.25
- dec_fc2: bfloat16 [2048, 512], replicated, may hold values from -0.125 to 0.125
- cotangent: bfloat16 [64, 1568, 512], P('dp', 'fsdp'), may hold values from -0.796875 to 0.796875
Outputs:
- grad_tokens: float32 [64, 157, 1408], P('dp', None, 'fsdp')
- grad_qkv: float32 [1408, 3, 1408], P('dp', None, 'fsdp')
- grad_proj: float32 [1408, 1408], P('fsdp', 'dp')
The draws below stay inside these ranges and needn't reach their ends.
Inputs may be any that keep to these rules, and one draw needn't show every extreme that they name: `vis_index`: each clip's row is strictly increasing. `owner`: in every clip's row each index of fsdp appears exactly 784 times.
All inputs are finite; a program needn't handle non-finite values.
Results may differ from the reference program's by a relative error of at most 0.02.
Values may be sent and summed in bfloat16 or wider, within the bound.
A program may use at most 192 MiB of HBM per device.

```python
import math
import jax
import jax.numpy as jnp
from jax import lax

D = 1408
HD = 88
EH = 16
ED = 1408
DD = 512
DHD = 64
DH = 4
DI = 256
DF = 2048
TUBES = 1568
VIS = 157
CLIPS = 64
OWN = 784


def qkv_weight(key, fan_in, width):
    normal_base = jax.random.normal(key, (fan_in, 3 * width), jnp.float32) * fan_in ** (-0.5)
    query_part = normal_base[:, :width]
    key_part = normal_base[:, width:2 * width]
    value_part = normal_base[:, 2 * width:]
    return jnp.concatenate([query_part, key_part, value_part], axis=1).astype(jnp.bfloat16)


def draw_enc_qkv(key, part):
    key = jax.random.fold_in(key, 37)
    return qkv_weight(key, D, ED).reshape(D, 3, ED)


def draw_dec_qkv(key, part):
    key = jax.random.fold_in(key, 41)
    return qkv_weight(key, DD, DI)


def draw_vis_index(key, part):
    key = jax.random.fold_in(key, 11)
    clip_keys = jax.random.split(key, CLIPS)

    def pick_visible(clip_key):
        return jax.random.permutation(clip_key, TUBES)[:VIS]
    chosen = jax.vmap(pick_visible)(clip_keys)
    return jnp.sort(chosen, axis=1).astype(jnp.int32)


def draw_owner(key, part):
    key = jax.random.fold_in(key, 23)
    clip_keys = jax.random.split(key, CLIPS)

    def arrange(clip_key):
        return (jax.random.permutation(clip_key, TUBES) // OWN).astype(jnp.int32)
    return jax.vmap(arrange)(clip_keys)


def raised(drawn, key, source, target, parts, factor):
    owner, partner = [(jnp.arange(drawn.shape[position]) // (drawn.shape[position] // parts)).reshape([-1 if axis == position else 1 for axis in range(drawn.ndim)]) for position in (source, target)]
    chosen = jax.random.permutation(key, parts)[partner]
    strong = (owner == chosen) | (owner == (partner + parts // 2) % parts)
    return jnp.where(strong, factor * drawn, drawn)


def block_scale(rng, dims, cuts, low, high):
    def one(dim, parts):
        steps = jax.random.uniform(jax.random.fold_in(jax.random.fold_in(rng, 6), dim), (parts,), jnp.float32, low / len(cuts), high / len(cuts))
        return jnp.repeat(jnp.exp(steps), dims[dim] // parts).reshape((-1,) + (1,) * (len(dims) - dim - 1))

    loudness = one(*cuts[0])
    for cut in cuts[1:]:
        loudness = loudness * one(*cut)
    return loudness


def gaussian(own_key, shape, deviation, reach, cuts=(), held_as=jnp.bfloat16):
    drawn = jax.random.normal(own_key, shape, jnp.float32) * deviation
    if len(cuts) > 0:
        drawn = block_scale(own_key, shape, cuts, -0.22, 0.18) * drawn
    return jnp.clip(drawn, min=-reach, max=reach).astype(held_as)


def heavy_noise(key, extent, deviation, limit, cuts, heavy, kind=jnp.bfloat16):
    values = deviation * jax.random.normal(key, extent, jnp.float32)
    if cuts:
        values = values * block_scale(key, extent, cuts, -0.22, 0.18)
    return jnp.clip(raised(values, jax.random.fold_in(key, 3), *heavy), -limit, limit).astype(kind)


def setup_inputs(seed: int = 0) -> dict:
    splits = jax.random.split(jax.random.key(seed), 16)
    return {
        "tokens": heavy_noise(splits[0], (CLIPS, VIS, D), 1.0, 16.0, ((0, 64), (2, 2)), (0, 2, 64, 4.0)),
        "vis_index": draw_vis_index(jax.random.fold_in(splits[15], 71), 0),
        "owner": draw_owner(jax.random.fold_in(splits[15], 71), 0),
        "enc_gain": jnp.clip(1.0 + 0.1 * jax.random.normal(splits[3], (D,), jnp.float32), 0.5, 1.5).astype(jnp.bfloat16),
        "enc_qkv": draw_enc_qkv(jax.random.fold_in(splits[15], 71), 0),
        "enc_proj": gaussian(splits[5], (ED, D), ED ** -0.5, 0.15625, ((0, 2),)),
        "to_decoder": gaussian(splits[6], (D, DD), D ** -0.5, 0.15625),
        "mask_token": gaussian(splits[7], (DD,), 1.0, 4.0),
        "dec_gain1": jnp.clip(1.0 + 0.1 * jax.random.normal(splits[8], (DD,), jnp.float32), 0.5, 1.5).astype(jnp.bfloat16),
        "dec_qkv": draw_dec_qkv(jax.random.fold_in(splits[15], 71), 0),
        "dec_proj": gaussian(splits[10], (DI, DD), DI ** -0.5, 0.375),
        "dec_gain2": jnp.clip(1.0 + 0.1 * jax.random.normal(splits[11], (DD,), jnp.float32), 0.5, 1.5).astype(jnp.bfloat16),
        "dec_fc1": gaussian(splits[12], (DD, DF), DD ** -0.5, 0.25),
        "dec_fc2": gaussian(splits[13], (DF, DD), DF ** -0.5, 0.125),
        "cotangent": gaussian(splits[14], (CLIPS, TUBES, DD), 0.1, 0.796875, ((0, 64), (1, 2))),
    }


EPS = 1e-06
SQRT_HALF = 0.7071067811865476
INV_SQRT_TWO_PI = 0.3989422804014327

def as_float(array):
    return array.astype(jnp.float32)

def norm_rows(values, gain_row):
    row_mean = lax.optimization_barrier(jnp.mean(values, axis=-1, keepdims=True))
    centred = values - row_mean
    inv_scale = lax.rsqrt(lax.optimization_barrier(jnp.mean(centred * centred, axis=-1, keepdims=True)) + EPS)
    normed = centred * inv_scale
    return (normed * gain_row, normed, inv_scale)

def norm_rows_back(grad_out, normed, inv_scale, gain_row):
    scaled = grad_out * gain_row
    first_mean = lax.optimization_barrier(jnp.mean(scaled, axis=-1, keepdims=True))
    second_mean = lax.optimization_barrier(jnp.mean(scaled * normed, axis=-1, keepdims=True))
    return inv_scale * (scaled - first_mean - normed * second_mean)

def gelu_slope(values):
    return 0.5 * (1.0 + lax.erf(values * SQRT_HALF)) + values * jnp.exp(-0.5 * values * values) * INV_SQRT_TWO_PI

def position_table(tube_ids, width):
    half_width = width // 2
    rates = jnp.exp(jnp.arange(half_width, dtype=jnp.float32) * (-2.0 * math.log(10000.0) / width))
    angles = tube_ids.astype(jnp.float32)[..., None] * rates
    return jnp.stack([jnp.sin(angles), jnp.cos(angles)], axis=-1).reshape(tube_ids.shape + (width,))

def encoder_forward(tokens_clip, gain_row, weight_qkv, weight_proj, weight_down):
    values = as_float(tokens_clip)
    gained, normed, inv_scale = norm_rows(values, gain_row)
    hidden = gained.astype(jnp.bfloat16)
    qkv_rows = jnp.dot(hidden, weight_qkv, preferred_element_type=jnp.float32)
    query_rows = (qkv_rows[:, :ED] * HD ** (-0.5)).astype(jnp.bfloat16).reshape(VIS, EH, HD)
    key_rows = qkv_rows[:, ED:2 * ED].astype(jnp.bfloat16).reshape(VIS, EH, HD)
    value_rows = qkv_rows[:, 2 * ED:].astype(jnp.bfloat16).reshape(VIS, EH, HD)
    scores = jnp.einsum('qhd,khd->hqk', as_float(query_rows), as_float(key_rows))
    enc_probs = jax.nn.softmax(scores, axis=-1)
    probs_low = enc_probs.astype(jnp.bfloat16)
    mixed_rows = jnp.einsum('hqk,khd->qhd', as_float(probs_low), as_float(value_rows)).astype(jnp.bfloat16).reshape(VIS, ED)
    encoded = (values + jnp.dot(mixed_rows, weight_proj, preferred_element_type=jnp.float32)).astype(jnp.bfloat16)
    lowered = jnp.dot(encoded, weight_down, preferred_element_type=jnp.float32).astype(jnp.bfloat16)
    return (lowered, (hidden, normed, inv_scale, query_rows, key_rows, value_rows, enc_probs, probs_low, mixed_rows))

def encoder_backward(grad_lowered, gain_row, weight_qkv, weight_proj, weight_down, saved_parts):
    hidden, normed, inv_scale, query_rows, key_rows, value_rows, enc_probs, probs_low, mixed_rows = saved_parts
    grad_encoded = jnp.dot(grad_lowered, weight_down.T, preferred_element_type=jnp.float32)
    grad_encoded_low = grad_encoded.astype(jnp.bfloat16)
    grad_mix = jnp.dot(grad_encoded_low, weight_proj.T, preferred_element_type=jnp.float32).astype(jnp.bfloat16).reshape(VIS, EH, HD)
    grad_probs = jnp.einsum('qhd,khd->hqk', as_float(grad_mix), as_float(value_rows))
    centre = lax.optimization_barrier(jnp.sum(enc_probs * grad_probs, axis=-1, keepdims=True))
    grad_scores = (enc_probs * (grad_probs - centre)).astype(jnp.bfloat16)
    grad_query = jnp.einsum('hqk,khd->qhd', as_float(grad_scores), as_float(key_rows)).reshape(VIS, ED)
    grad_keys = jnp.einsum('hqk,qhd->khd', as_float(grad_scores), as_float(query_rows)).reshape(VIS, ED)
    grad_values = jnp.einsum('hqk,qhd->khd', as_float(probs_low), as_float(grad_mix)).reshape(VIS, ED)
    grad_qkv_rows = jnp.concatenate([grad_query * HD ** (-0.5), grad_keys, grad_values], axis=-1).astype(jnp.bfloat16)
    grad_hidden = jnp.dot(grad_qkv_rows, weight_qkv.T, preferred_element_type=jnp.float32)
    grad_tokens = grad_encoded + norm_rows_back(grad_hidden, normed, inv_scale, gain_row)
    return (grad_tokens, hidden, grad_qkv_rows, mixed_rows, grad_encoded_low)

def decoder_clip(lowered, visible, owners, cotangent_rows, params):
    mask_row, gain_one, weight_qkv, weight_proj, gain_two, weight_up, weight_out = params
    slot_tubes = jnp.argsort(owners, stable=True).astype(jnp.int32)
    hit_table = slot_tubes[:, None] == visible[None, :]
    hits_low = hit_table.astype(jnp.bfloat16)
    placed = jnp.dot(hits_low, lowered, preferred_element_type=jnp.float32)
    covered = lax.optimization_barrier(jnp.sum(hit_table.astype(jnp.float32), axis=1, keepdims=True))
    start_rows = (placed + (1.0 - covered) * mask_row + position_table(slot_tubes, DD)).astype(jnp.bfloat16)
    x_start = as_float(start_rows)
    gained_one, normed_one, inv_one = norm_rows(x_start, gain_one)
    attn_in = gained_one.astype(jnp.bfloat16)
    dec_mix = jnp.dot(attn_in, weight_qkv, preferred_element_type=jnp.float32)
    query_rows = (dec_mix[:, :DI] * DHD ** (-0.5)).astype(jnp.bfloat16).reshape(TUBES, DH, DHD)
    key_rows = dec_mix[:, DI:2 * DI].astype(jnp.bfloat16).reshape(TUBES, DH, DHD)
    value_rows = dec_mix[:, 2 * DI:].astype(jnp.bfloat16).reshape(TUBES, DH, DHD)
    scores = jnp.einsum('qhd,khd->hqk', as_float(query_rows), as_float(key_rows))
    dec_probs = jax.nn.softmax(scores, axis=-1)
    probs_low = dec_probs.astype(jnp.bfloat16)
    mixed_rows = jnp.einsum('hqk,khd->qhd', as_float(probs_low), as_float(value_rows)).astype(jnp.bfloat16).reshape(TUBES, DI)
    after_attn = (x_start + jnp.dot(mixed_rows, weight_proj, preferred_element_type=jnp.float32)).astype(jnp.bfloat16)
    gained_two, normed_two, inv_two = norm_rows(as_float(after_attn), gain_two)
    mlp_in = gained_two.astype(jnp.bfloat16)
    up_proj = jnp.dot(mlp_in, weight_up, preferred_element_type=jnp.float32)
    grad_act = jnp.dot(cotangent_rows, weight_out.T, preferred_element_type=jnp.float32)
    grad_up = (grad_act * gelu_slope(up_proj)).astype(jnp.bfloat16)
    grad_mlp_in = jnp.dot(grad_up, weight_up.T, preferred_element_type=jnp.float32)
    grad_mid = as_float(cotangent_rows) + norm_rows_back(grad_mlp_in, normed_two, inv_two, gain_two)
    grad_mid_low = grad_mid.astype(jnp.bfloat16)
    grad_mix = jnp.dot(grad_mid_low, weight_proj.T, preferred_element_type=jnp.float32).astype(jnp.bfloat16).reshape(TUBES, DH, DHD)
    grad_probs = jnp.einsum('qhd,khd->hqk', as_float(grad_mix), as_float(value_rows))
    centre = lax.optimization_barrier(jnp.sum(dec_probs * grad_probs, axis=-1, keepdims=True))
    grad_scores = (dec_probs * (grad_probs - centre)).astype(jnp.bfloat16)
    grad_query = jnp.einsum('hqk,khd->qhd', as_float(grad_scores), as_float(key_rows)).reshape(TUBES, DI)
    grad_keys = jnp.einsum('hqk,qhd->khd', as_float(grad_scores), as_float(query_rows)).reshape(TUBES, DI)
    grad_values = jnp.einsum('hqk,qhd->khd', as_float(probs_low), as_float(grad_mix)).reshape(TUBES, DI)
    grad_qkv_rows = jnp.concatenate([grad_query * DHD ** (-0.5), grad_keys, grad_values], axis=-1).astype(jnp.bfloat16)
    grad_attn_in = jnp.dot(grad_qkv_rows, weight_qkv.T, preferred_element_type=jnp.float32)
    grad_start = grad_mid + norm_rows_back(grad_attn_in, normed_one, inv_one, gain_one)
    grad_start_low = grad_start.astype(jnp.bfloat16)
    return jnp.dot(hits_low.T, grad_start_low, preferred_element_type=jnp.float32).astype(jnp.bfloat16)

def reference(tokens, vis_index, owner, enc_gain, enc_qkv, enc_proj, to_decoder, mask_token, dec_gain1, dec_qkv, dec_proj, dec_gain2, dec_fc1, dec_fc2, cotangent):
    gain_enc = as_float(enc_gain)
    flat_qkv = enc_qkv.reshape(D, 3 * ED)

    def forward_clip(tokens_clip):
        return encoder_forward(tokens_clip, gain_enc, flat_qkv, enc_proj, to_decoder)
    lowered, saved_parts = lax.map(forward_clip, tokens)
    params = (as_float(mask_token), as_float(dec_gain1), dec_qkv, dec_proj, as_float(dec_gain2), dec_fc1, dec_fc2)

    def decode_clip(inputs):
        lowered_clip, visible, owners, cot_clip = inputs
        return decoder_clip(lowered_clip, visible, owners, cot_clip, params)
    grad_lowered = lax.map(decode_clip, (lowered, vis_index, owner, cotangent))

    def backward_clip(inputs):
        grad_clip, saved_clip = inputs
        return encoder_backward(grad_clip, gain_enc, flat_qkv, enc_proj, to_decoder, saved_clip)
    grad_tokens, hidden, grad_qkv_rows, mixed_rows, grad_encoded_low = lax.map(backward_clip, (grad_lowered, saved_parts))
    grad_qkv = jnp.dot(hidden.reshape(-1, D).T, grad_qkv_rows.reshape(-1, 3 * ED), preferred_element_type=jnp.float32)
    grad_proj = jnp.dot(mixed_rows.reshape(-1, ED).T, grad_encoded_low.reshape(-1, D), preferred_element_type=jnp.float32)
    return (grad_tokens, grad_qkv.reshape(D, 3, ED), grad_proj)
```

```python
import functools
import math

import jax
import jax.numpy as jnp
import numpy as np
from jax import lax
from jax.experimental import pallas as pl
from jax.experimental.pallas import tpu as pltpu
from jax.sharding import PartitionSpec as P

D = 1408
HALF = 704
HD = 88
HEADS = 8
DD = 512
DHD = 64
DH = 4
DI = 256
DF = 2048
TUBES = 1568
VIS = 157
ROWS = 160
OWN = 784
BLK = 112
EPS = 1e-06
ENC_SCALE = HD ** (-0.5)
DEC_SCALE = DHD ** (-0.5)
SQRT_HALF = 0.7071067811865476
INV_SQRT_TWO_PI = 0.3989422804014327
F32 = jnp.float32
BF16 = jnp.bfloat16
MESH = pl.DeviceIdType.MESH


def nn(a, b):
    return lax.dot_general(a, b, (((1,), (0,)), ((), ())), preferred_element_type=F32)


def nt(a, b):
    return lax.dot_general(a, b, (((1,), (1,)), ((), ())), preferred_element_type=F32)


def tn(a, b):
    return lax.dot_general(a, b, (((0,), (0,)), ((), ())), preferred_element_type=F32)


def norm_parts(values, width):
    mean = jnp.sum(values, axis=-1, keepdims=True) * (1.0 / width)
    centred = values - mean
    inv = lax.rsqrt(jnp.sum(centred * centred, axis=-1, keepdims=True) * (1.0 / width) + EPS)
    return centred * inv, inv


def norm_back(grad, normed, inv, gain, width):
    scaled = grad * gain
    first = jnp.sum(scaled, axis=-1, keepdims=True) * (1.0 / width)
    second = jnp.sum(scaled * normed, axis=-1, keepdims=True) * (1.0 / width)
    return inv * (scaled - first - normed * second)


def gelu_slope(u):
    e = jnp.exp(u * u * -0.5)
    t = 1.0 / (1.0 + (0.3275911 * SQRT_HALF) * jnp.abs(u))
    poly = t * (0.254829592 + t * (-0.284496736 + t * (1.421413741 + t * (-1.453152027 + t * 1.061405429))))
    tail = (0.5 * e) * poly
    return jnp.where(u >= 0.0, 1.0 - tail, tail) + u * e * INV_SQRT_TWO_PI


def position_rows():
    rates = np.exp(np.arange(DD // 2, dtype=np.float32) * np.float32(-2.0 * math.log(10000.0) / DD))
    angles = np.arange(TUBES, dtype=np.float32)[:, None] * rates
    return np.stack([np.sin(angles), np.cos(angles)], axis=-1).reshape(TUBES, DD).astype(np.float32)


def main_kernel(
    tok, visr, visc, rank, genc, maskt, gain1, gain2,
    wt_h, proj_h, down_h, dqkv_h, dproj_h, fc1_h, fc2_h, cot_h, pos_h,
    gtok, hid_o, gqkv_o, mixed_o, gel_o,
    wt, proj, down, dqkv, dproj, fc1, fc2, cot, pos,
    tokpad, tokrecv, xfull, invs, qs, ks, vs, lows, lowr,
    xall, kd, vd, xown, qd, mixd, mxs, lis, mlp, acc, gmid, gmix, cen,
    exs, exr, hts, htr, sts, strr,
    local, send, recv,
):
    me = lax.axis_index("fsdp")
    other = 1 - me
    first = me == 0

    loads = [
        pltpu.make_async_copy(src, dst, local.at[i])
        for i, (src, dst) in enumerate(
            [(wt_h, wt), (pos_h, pos), (proj_h, proj), (down_h, down), (dqkv_h, dqkv),
             (dproj_h, dproj), (fc1_h, fc1), (fc2_h, fc2), (cot_h, cot)]
        )
    ]
    for load in loads:
        load.start()
    l_wt, l_pos, l_proj, l_down, l_dqkv, l_dproj, l_fc1, l_fc2, l_cot = loads

    def exchange(src, dst, i):
        return pltpu.make_async_remote_copy(
            src_ref=src, dst_ref=dst, send_sem=send.at[i], recv_sem=recv.at[i],
            device_id={"fsdp": other}, device_id_type=MESH,
        )

    barrier = pltpu.get_barrier_semaphore()
    pl.semaphore_signal(barrier, inc=1, device_id={"fsdp": other}, device_id_type=MESH)

    tokpad[...] = jnp.zeros((ROWS, HALF), BF16)
    tokpad[0:VIS, :] = tok[...]
    pl.semaphore_wait(barrier, 1)
    swap = exchange(tokpad, tokrecv, 0)
    swap.start()

    vis_row = visr[...]
    vis_col = visc[...]
    lane_tube = lax.broadcasted_iota(jnp.int32, (ROWS, TUBES), 1)
    vis_hit = lane_tube == vis_col
    vis_pick = vis_hit.astype(F32).astype(BF16)
    slot_of = jnp.sum(jnp.where(vis_hit, rank[...] + 1, 0), axis=1, keepdims=True) - 1
    own_pick = (lax.broadcasted_iota(jnp.int32, (ROWS, OWN), 1) == slot_of).astype(F32).astype(BF16)

    swap.wait()
    mine = tokpad[...].astype(F32)
    theirs = tokrecv[...].astype(F32)
    xfull[:, 0:HALF] = jnp.where(first, mine, theirs)
    xfull[:, HALF:D] = jnp.where(first, theirs, mine)
    values = xfull[...]
    normed, inv = norm_parts(values, D)
    invs[...] = inv
    gain_enc = genc[...].astype(F32)
    hidden = (normed * gain_enc).astype(BF16)
    hid_o[...] = hidden
    l_wt.wait()
    qs[...] = (nt(hidden, wt[0:HALF, :]) * ENC_SCALE).astype(BF16)
    ks[...] = nt(hidden, wt[HALF:2 * HALF, :]).astype(BF16)
    vs[...] = nt(hidden, wt[2 * HALF:3 * HALF, :]).astype(BF16)
    key_ok = lax.broadcasted_iota(jnp.int32, (ROWS, ROWS), 1) < VIS

    def enc_probs(h):
        lanes = slice(h * HD, (h + 1) * HD)
        s = nt(qs[:, lanes], ks[:, lanes])
        s = jnp.where(key_ok, s, -1e30)
        e = jnp.exp(s - jnp.max(s, axis=-1, keepdims=True))
        return e / jnp.sum(e, axis=-1, keepdims=True)

    for h in range(HEADS):
        lanes = slice(h * HD, (h + 1) * HD)
        mixed_o[:, lanes] = nn(enc_probs(h).astype(BF16), vs[:, lanes]).astype(BF16)
    l_proj.wait()
    heads_term = nn(mixed_o[...], proj[...])
    part_enc = (jnp.where(first, xfull[...], 0.0) + heads_term).astype(BF16)
    l_down.wait()
    lows[...] = nn(part_enc, down[...])
    swap = exchange(lows, lowr, 1)
    swap.start()

    swap.wait()
    lowered = (lows[...] + lowr[...]).astype(BF16)
    l_pos.wait()
    l_dqkv.wait()
    gain_one = gain1[...].astype(F32)
    gain_two = gain2[...].astype(F32)
    mask_row = maskt[...].astype(F32)

    @pl.loop(0, TUBES // BLK)
    def _(b):
        rows = pl.ds(pl.multiple_of(b * BLK, BLK), BLK)
        hit = lax.broadcasted_iota(jnp.int32, (BLK, ROWS), 0) + b * BLK == vis_row
        hit = hit.astype(F32)
        placed = nn(hit.astype(BF16), lowered)
        covered = jnp.sum(hit, axis=1, keepdims=True)
        start = (placed + (1.0 - covered) * mask_row + pos[rows, :]).astype(BF16)
        xall[rows, :] = start
        n1, _ = norm_parts(start.astype(F32), DD)
        attn_in = (n1 * gain_one).astype(BF16)
        kv = nn(attn_in, dqkv[:, DI:3 * DI]).astype(BF16)
        for h in range(DH):
            kd[h, rows, :] = kv[:, h * DHD:(h + 1) * DHD]
            vd[h, rows, :] = kv[:, DI + h * DHD:DI + (h + 1) * DHD]

    @pl.loop(0, OWN // BLK)
    def _(b):
        rows = pl.ds(pl.multiple_of(b * BLK, BLK), BLK)
        pick = lax.broadcasted_iota(jnp.int32, (BLK, TUBES), 0) + b * BLK == rank[...]
        start = nn(pick.astype(F32).astype(BF16), xall[...])
        xown[rows, :] = start
        n1, _ = norm_parts(start, DD)
        attn_in = (n1 * gain_one).astype(BF16)
        q = (nn(attn_in, dqkv[:, 0:DI]) * DEC_SCALE).astype(BF16)
        for h in range(DH):
            qd[h, rows, :] = q[:, h * DHD:(h + 1) * DHD]

    @pl.loop(0, OWN // BLK)
    def _(b):
        rows = pl.ds(pl.multiple_of(b * BLK, BLK), BLK)
        for h in range(DH):
            s = nt(qd[h, rows, :], kd[h])
            top = jnp.max(s, axis=-1, keepdims=True)
            e = jnp.exp(s - top)
            total = 1.0 / jnp.sum(e, axis=-1, keepdims=True)
            mxs[h, rows, :] = top
            lis[h, rows, :] = total
            mixd[rows, h * DHD:(h + 1) * DHD] = nn(e.astype(BF16), vd[h]) * total

    l_dproj.wait()

    def after(rows):
        return (xown[rows, :] + nn(mixd[rows, :].astype(BF16), dproj[...])).astype(BF16).astype(F32)

    @pl.loop(0, OWN // BLK)
    def _(b):
        rows = pl.ds(pl.multiple_of(b * BLK, BLK), BLK)
        n2, _ = norm_parts(after(rows), DD)
        mlp[rows, :] = (n2 * gain_two).astype(BF16)

    l_fc1.wait()
    l_fc2.wait()
    l_cot.wait()
    acc[...] = jnp.zeros((OWN, DD), F32)

    @pl.loop(0, DF // 256)
    def _(c):
        part = pl.ds(pl.multiple_of(c * 256, 256), 256)
        up = nn(mlp[...], fc1[:, part])
        gact = nt(cot[...], fc2[part, :])
        gup = (gact * gelu_slope(up)).astype(BF16)
        acc[...] += nt(gup, fc1[:, part])

    @pl.loop(0, OWN // BLK)
    def _(b):
        rows = pl.ds(pl.multiple_of(b * BLK, BLK), BLK)
        n2, inv2 = norm_parts(after(rows), DD)
        g = cot[rows, :].astype(F32) + norm_back(acc[rows, :], n2, inv2, gain_two, DD)
        low = g.astype(BF16)
        gmid[rows, :] = low
        gm = nt(low, dproj[...]).astype(BF16)
        prod = gm.astype(F32) * mixd[rows, :]
        for h in range(DH):
            lanes = slice(h * DHD, (h + 1) * DHD)
            gmix[h, rows, :] = gm[:, lanes]
            cen[h, rows, :] = jnp.sum(prod[:, lanes], axis=-1, keepdims=True)

    vis_x = nn(vis_pick, xall[...])
    exs[:, 3 * DI:] = nn(own_pick, gmid[...]).astype(BF16)
    for h in range(DH):
        lanes = slice(h * DHD, (h + 1) * DHD)
        k_vis = nn(vis_pick, kd[h]).astype(BF16)
        v_vis = nn(vis_pick, vd[h]).astype(BF16)
        p = jnp.exp(nt(qd[h], k_vis) - mxs[h]) * lis[h]
        ds = (p * (nt(gmix[h], v_vis) - cen[h])).astype(BF16)
        exs[:, DI + h * DHD:DI + (h + 1) * DHD] = tn(ds, qd[h]).astype(BF16)
        exs[:, 2 * DI + h * DHD:2 * DI + (h + 1) * DHD] = tn(p.astype(BF16), gmix[h]).astype(BF16)
        q_vis = nn(own_pick, qd[h]).astype(BF16)
        g_vis = nn(own_pick, gmix[h]).astype(BF16)
        s = nt(q_vis, kd[h])
        e = jnp.exp(s - jnp.max(s, axis=-1, keepdims=True))
        p = e * (1.0 / jnp.sum(e, axis=-1, keepdims=True))
        g = nt(g_vis, vd[h])
        c = jnp.sum(p * g, axis=-1, keepdims=True)
        ds = (p * (g - c)).astype(BF16)
        exs[:, lanes] = (nn(ds, kd[h]) * DEC_SCALE).astype(BF16)

    swap = exchange(exs, exr, 2)
    swap.start()
    swap.wait()
    both = exs[...].astype(F32) + exr[...].astype(F32)
    gattn = nt(both[:, 0:3 * DI].astype(BF16), dqkv[...])
    n1, inv1 = norm_parts(vis_x, DD)
    gstart = both[:, 3 * DI:] + norm_back(gattn, n1, inv1, gain_one, DD)
    real = lax.broadcasted_iota(jnp.int32, (ROWS, DD), 0) < VIS
    glow = jnp.where(real, gstart, 0.0).astype(BF16)

    genc_rows = nt(glow, down[...])
    gel = genc_rows.astype(BF16)
    gel_o[...] = gel
    xfull[...] = genc_rows
    gmx = nt(gel, proj[...]).astype(BF16)
    for h in range(HEADS):
        lanes = slice(h * HD, (h + 1) * HD)
        p = enc_probs(h)
        gm = gmx[:, lanes]
        g = nt(gm, vs[:, lanes])
        c = jnp.sum(p * g, axis=-1, keepdims=True)
        ds = (p * (g - c)).astype(BF16)
        gqkv_o[:, h * HD:(h + 1) * HD] = (nn(ds, ks[:, lanes]) * ENC_SCALE).astype(BF16)
        gqkv_o[:, HALF + h * HD:HALF + (h + 1) * HD] = tn(ds, qs[:, lanes]).astype(BF16)
        gqkv_o[:, 2 * HALF + h * HD:2 * HALF + (h + 1) * HD] = tn(p.astype(BF16), gm).astype(BF16)
    terms = nn(gqkv_o[...], wt[...]).astype(BF16)
    scaled = terms.astype(F32) * gain_enc
    mine = tokpad[...].astype(F32)
    theirs = tokrecv[...].astype(F32)
    full = jnp.concatenate([jnp.where(first, mine, theirs), jnp.where(first, theirs, mine)], axis=1)
    normed, inv = norm_parts(full, D)
    s1 = jnp.sum(scaled, axis=-1, keepdims=True)
    s2 = jnp.sum(scaled * normed, axis=-1, keepdims=True)
    sts[...] = jnp.where(lax.broadcasted_iota(jnp.int32, (ROWS, 128), 1) == 0, s1, s2)
    hts[...] = jnp.where(first, terms[:, HALF:], terms[:, 0:HALF])
    swap_a = exchange(hts, htr, 3)
    swap_b = exchange(sts, strr, 4)
    swap_a.start()
    swap_b.start()
    swap_a.wait()
    swap_b.wait()
    stats = sts[...] + strr[...]
    m1 = stats[:, 0:1] * (1.0 / D)
    m2 = stats[:, 1:2] * (1.0 / D)
    gh = jnp.where(first, terms[:, 0:HALF], terms[:, HALF:]).astype(F32) + htr[...].astype(F32)
    gain_mine = jnp.where(first, gain_enc[:, 0:HALF], gain_enc[:, HALF:])
    normed_mine = jnp.where(first, normed[:, 0:HALF], normed[:, HALF:])
    base = jnp.where(first, xfull[:, 0:HALF], xfull[:, HALF:D])
    out = base + inv * (gh * gain_mine - m1 - normed_mine * m2)
    gtok[...] = out[0:VIS, :]


def run_main(tok, visr, visc, rank, genc, maskt, gain1, gain2, wt, proj, down, dqkv, dproj, fc1, fc2, cot, pos):
    vm = pl.BlockSpec(memory_space=pltpu.VMEM)
    hbm = pl.BlockSpec(memory_space=pl.ANY)
    V = pltpu.VMEM
    big = (wt, proj, down, dqkv, dproj, fc1, fc2, cot, pos)
    scratch = [V(a.shape, a.dtype) for a in big] + [
        V((ROWS, HALF), BF16), V((ROWS, HALF), BF16), V((ROWS, D), F32), V((ROWS, 1), F32),
        V((ROWS, HALF), BF16), V((ROWS, HALF), BF16), V((ROWS, HALF), BF16),
        V((ROWS, DD), F32), V((ROWS, DD), F32),
        V((TUBES, DD), BF16), V((DH, TUBES, DHD), BF16), V((DH, TUBES, DHD), BF16),
        V((OWN, DD), F32), V((DH, OWN, DHD), BF16), V((OWN, DI), F32),
        V((DH, OWN, 1), F32), V((DH, OWN, 1), F32),
        V((OWN, DD), BF16), V((OWN, DD), F32), V((OWN, DD), BF16),
        V((DH, OWN, DHD), BF16), V((DH, OWN, 1), F32),
        V((ROWS, 3 * DI + DD), BF16), V((ROWS, 3 * DI + DD), BF16),
        V((ROWS, HALF), BF16), V((ROWS, HALF), BF16), V((ROWS, 128), F32), V((ROWS, 128), F32),
        pltpu.SemaphoreType.DMA((9,)), pltpu.SemaphoreType.DMA((5,)), pltpu.SemaphoreType.DMA((5,)),
    ]
    return pl.pallas_call(
        main_kernel,
        out_shape=(
            jax.ShapeDtypeStruct((VIS, HALF), F32),
            jax.ShapeDtypeStruct((ROWS, D), BF16),
            jax.ShapeDtypeStruct((ROWS, 3 * HALF), BF16),
            jax.ShapeDtypeStruct((ROWS, HALF), BF16),
            jax.ShapeDtypeStruct((ROWS, D), BF16),
        ),
        in_specs=[vm] * 8 + [hbm] * 9,
        out_specs=[vm] * 5,
        scratch_shapes=scratch,
        compiler_params=pltpu.CompilerParams(
            collective_id=0, has_side_effects=True, vmem_limit_bytes=60 * 1024 * 1024
        ),
    )(tok, visr, visc, rank, genc, maskt, gain1, gain2, *big)


def per_device(
    tokens, vis_index, owner, enc_gain, enc_qkv, enc_proj, to_decoder, mask_token, dec_gain1,
    dec_qkv, dec_proj, dec_gain2, dec_fc1, dec_fc2, cotangent,
):
    me = lax.axis_index("fsdp")
    mine = (owner == me).astype(jnp.int32)
    rank = jnp.where(mine == 1, jnp.cumsum(mine, axis=1) - 1, -1)
    vis = jnp.pad(vis_index, ((0, 0), (0, ROWS - VIS)), constant_values=-1)
    wt = jnp.transpose(enc_qkv, (1, 2, 0)).reshape(3 * HALF, D)
    gtok, hidden, gqkv, mixed, gel = run_main(
        tokens[0], vis, vis.reshape(ROWS, 1), rank, enc_gain[None], mask_token[None],
        dec_gain1[None], dec_gain2[None], wt, enc_proj, to_decoder, dec_qkv, dec_proj,
        dec_fc1, dec_fc2, cotangent[0], jnp.asarray(position_rows()),
    )
    qkv_term = jnp.dot(hidden.T, gqkv, preferred_element_type=F32).reshape(D, 3, HALF)
    proj_term = jnp.dot(mixed.T, gel, preferred_element_type=F32)
    return (
        gtok[None],
        lax.psum_scatter(qkv_term, "dp", scatter_dimension=0, tiled=True),
        lax.psum_scatter(proj_term, "dp", scatter_dimension=1, tiled=True),
    )


def solution(mesh):
    return jax.shard_map(
        per_device,
        mesh=mesh,
        in_specs=(
            P("dp", None, "fsdp"),
            P("dp", None),
            P("dp", None),
            P(),
            P(None, None, "fsdp"),
            P("fsdp", None),
            P(),
            P(),
            P(),
            P(),
            P(),
            P(),
            P(),
            P(),
            P("dp", "fsdp", None),
        ),
        out_specs=(P("dp", None, "fsdp"), P("dp", None, "fsdp"), P("fsdp", "dp")),
        check_vma=False,
    )
```

```python
import functools
import math

import jax
import jax.numpy as jnp
import numpy as np
from jax import lax
from jax.experimental import pallas as pl
from jax.experimental.pallas import tpu as pltpu
from jax.sharding import PartitionSpec as P

D = 1408
HALF = 704
HD = 88
HEADS = 8
DD = 512
DHD = 64
DH = 4
DI = 256
DF = 2048
TUBES = 1568
VIS = 157
ROWS = 160
OWN = 784
BLK = 112
EPS = 1e-06
ENC_SCALE = HD ** (-0.5)
DEC_SCALE = DHD ** (-0.5)
SQRT_HALF = 0.7071067811865476
INV_SQRT_TWO_PI = 0.3989422804014327
F32 = jnp.float32
BF16 = jnp.bfloat16
MESH = pl.DeviceIdType.MESH


def nn(a, b):
    return lax.dot_general(a, b, (((1,), (0,)), ((), ())), preferred_element_type=F32)


def nt(a, b):
    return lax.dot_general(a, b, (((1,), (1,)), ((), ())), preferred_element_type=F32)


def tn(a, b):
    return lax.dot_general(a, b, (((0,), (0,)), ((), ())), preferred_element_type=F32)


def norm_parts(values, width):
    mean = jnp.sum(values, axis=-1, keepdims=True) * (1.0 / width)
    centred = values - mean
    inv = lax.rsqrt(jnp.sum(centred * centred, axis=-1, keepdims=True) * (1.0 / width) + EPS)
    return centred * inv, inv


def norm_back(grad, normed, inv, gain, width):
    scaled = grad * gain
    first = jnp.sum(scaled, axis=-1, keepdims=True) * (1.0 / width)
    second = jnp.sum(scaled * normed, axis=-1, keepdims=True) * (1.0 / width)
    return inv * (scaled - first - normed * second)


def gelu_slope(u):
    e = jnp.exp(u * u * -0.5)
    t = 1.0 / (1.0 + (0.3275911 * SQRT_HALF) * jnp.abs(u))
    poly = t * (0.254829592 + t * (-0.284496736 + t * (1.421413741 + t * (-1.453152027 + t * 1.061405429))))
    tail = (0.5 * e) * poly
    return jnp.where(u >= 0.0, 1.0 - tail, tail) + u * e * INV_SQRT_TWO_PI


def position_rows():
    rates = np.exp(np.arange(DD // 2, dtype=np.float32) * np.float32(-2.0 * math.log(10000.0) / DD))
    angles = np.arange(TUBES, dtype=np.float32)[:, None] * rates
    return np.stack([np.sin(angles), np.cos(angles)], axis=-1).reshape(TUBES, DD).astype(np.float32)


def main_kernel(
    tok, visr, visc, rank, genc, maskt, gain1, gain2,
    wt_h, proj_h, down_h, dqkv_h, dproj_h, fc1_h, fc2_h, cot_h, pos_h,
    gtok, hid_o, gqkv_o, mixed_o, gel_o,
    wt, proj, down, dqkv, dproj, fc1, fc2, cot, pos,
    tokpad, tokrecv, xfull, invs, qs, ks, vs, lows, lowr,
    xall, kd, vd, xown, qd, mixd, mxs, lis, mlp, acc, gmid, gmix, cen,
    exs, exr, hts, htr, sts, strr,
    local, send, recv,
):
    me = lax.axis_index("fsdp")
    other = 1 - me
    first = me == 0

    loads = [
        pltpu.make_async_copy(src, dst, local.at[i])
        for i, (src, dst) in enumerate(
            [(wt_h, wt), (pos_h, pos), (proj_h, proj), (down_h, down), (dqkv_h, dqkv),
             (dproj_h, dproj), (fc1_h, fc1), (fc2_h, fc2), (cot_h, cot)]
        )
    ]
    for load in loads:
        load.start()
    l_wt, l_pos, l_proj, l_down, l_dqkv, l_dproj, l_fc1, l_fc2, l_cot = loads

    def exchange(src, dst, i):
        return pltpu.make_async_remote_copy(
            src_ref=src, dst_ref=dst, send_sem=send.at[i], recv_sem=recv.at[i],
            device_id={"fsdp": other}, device_id_type=MESH,
        )

    barrier = pltpu.get_barrier_semaphore()
    pl.semaphore_signal(barrier, inc=1, device_id={"fsdp": other}, device_id_type=MESH)

    tokpad[...] = jnp.zeros((ROWS, HALF), BF16)
    tokpad[0:VIS, :] = tok[...]
    pl.semaphore_wait(barrier, 1)
    swap = exchange(tokpad, tokrecv, 0)
    swap.start()

    vis_row = visr[...]
    vis_col = visc[...]
    lane_tube = lax.broadcasted_iota(jnp.int32, (ROWS, TUBES), 1)
    vis_hit = lane_tube == vis_col
    vis_pick = vis_hit.astype(F32).astype(BF16)
    slot_of = jnp.sum(jnp.where(vis_hit, rank[...] + 1, 0), axis=1, keepdims=True) - 1
    own_pick = (lax.broadcasted_iota(jnp.int32, (ROWS, OWN), 1) == slot_of).astype(F32).astype(BF16)

    swap.wait()
    mine = tokpad[...].astype(F32)
    theirs = tokrecv[...].astype(F32)
    xfull[:, 0:HALF] = jnp.where(first, mine, theirs)
    xfull[:, HALF:D] = jnp.where(first, theirs, mine)
    values = xfull[...]
    normed, inv = norm_parts(values, D)
    invs[...] = inv
    gain_enc = genc[...].astype(F32)
    hidden = (normed * gain_enc).astype(BF16)
    hid_o[...] = hidden
    l_wt.wait()
    qs[...] = (nt(hidden, wt[0:HALF, :]) * ENC_SCALE).astype(BF16)
    ks[...] = nt(hidden, wt[HALF:2 * HALF, :]).astype(BF16)
    vs[...] = nt(hidden, wt[2 * HALF:3 * HALF, :]).astype(BF16)
    key_ok = lax.broadcasted_iota(jnp.int32, (ROWS, ROWS), 1) < VIS

    def enc_probs(h):
        lanes = slice(h * HD, (h + 1) * HD)
        s = nt(qs[:, lanes], ks[:, lanes])
        s = jnp.where(key_ok, s, -1e30)
        e = jnp.exp(s - jnp.max(s, axis=-1, keepdims=True))
        return e / jnp.sum(e, axis=-1, keepdims=True)

    for h in range(HEADS):
        lanes = slice(h * HD, (h + 1) * HD)
        mixed_o[:, lanes] = nn(enc_probs(h).astype(BF16), vs[:, lanes]).astype(BF16)
    l_proj.wait()
    heads_term = nn(mixed_o[...], proj[...])
    part_enc = (jnp.where(first, xfull[...], 0.0) + heads_term).astype(BF16)
    l_down.wait()
    lows[...] = nn(part_enc, down[...])
    swap = exchange(lows, lowr, 1)
    swap.start()

    swap.wait()
    lowered = (lows[...] + lowr[...]).astype(BF16)
    l_pos.wait()
    l_dqkv.wait()
    gain_one = gain1[...].astype(F32)
    gain_two = gain2[...].astype(F32)
    mask_row = maskt[...].astype(F32)

    @pl.loop(0, TUBES // BLK)
    def _(b):
        rows = pl.ds(pl.multiple_of(b * BLK, BLK), BLK)
        hit = lax.broadcasted_iota(jnp.int32, (BLK, ROWS), 0) + b * BLK == vis_row
        hit = hit.astype(F32)
        placed = nn(hit.astype(BF16), lowered)
        covered = jnp.sum(hit, axis=1, keepdims=True)
        start = (placed + (1.0 - covered) * mask_row + pos[rows, :]).astype(BF16)
        xall[rows, :] = start
        n1, _ = norm_parts(start.astype(F32), DD)
        attn_in = (n1 * gain_one).astype(BF16)
        kv = nn(attn_in, dqkv[:, DI:3 * DI]).astype(BF16)
        for h in range(DH):
            kd[h, rows, :] = kv[:, h * DHD:(h + 1) * DHD]
            vd[h, rows, :] = kv[:, DI + h * DHD:DI + (h + 1) * DHD]

    @pl.loop(0, OWN // BLK)
    def _(b):
        rows = pl.ds(pl.multiple_of(b * BLK, BLK), BLK)
        pick = lax.broadcasted_iota(jnp.int32, (BLK, TUBES), 0) + b * BLK == rank[...]
        start = nn(pick.astype(F32).astype(BF16), xall[...])
        xown[rows, :] = start
        n1, _ = norm_parts(start, DD)
        attn_in = (n1 * gain_one).astype(BF16)
        q = (nn(attn_in, dqkv[:, 0:DI]) * DEC_SCALE).astype(BF16)
        for h in range(DH):
            qd[h, rows, :] = q[:, h * DHD:(h + 1) * DHD]

    @pl.loop(0, OWN // BLK)
    def _(b):
        rows = pl.ds(pl.multiple_of(b * BLK, BLK), BLK)
        for h in range(DH):
            s = nt(qd[h, rows, :], kd[h])
            top = jnp.max(s, axis=-1, keepdims=True)
            e = jnp.exp(s - top)
            total = 1.0 / jnp.sum(e, axis=-1, keepdims=True)
            mxs[h, rows, :] = top
            lis[h, rows, :] = total
            mixd[rows, h * DHD:(h + 1) * DHD] = nn(e.astype(BF16), vd[h]) * total

    l_dproj.wait()

    def after(rows):
        return (xown[rows, :] + nn(mixd[rows, :].astype(BF16), dproj[...])).astype(BF16).astype(F32)

    @pl.loop(0, OWN // BLK)
    def _(b):
        rows = pl.ds(pl.multiple_of(b * BLK, BLK), BLK)
        n2, _ = norm_parts(after(rows), DD)
        mlp[rows, :] = (n2 * gain_two).astype(BF16)

    l_fc1.wait()
    l_fc2.wait()
    l_cot.wait()
    acc[...] = jnp.zeros((OWN, DD), F32)

    @pl.loop(0, DF // 256)
    def _(c):
        part = pl.ds(pl.multiple_of(c * 256, 256), 256)
        up = nn(mlp[...], fc1[:, part])
        gact = nt(cot[...], fc2[part, :])
        gup = (gact * gelu_slope(up)).astype(BF16)
        acc[...] += nt(gup, fc1[:, part])

    @pl.loop(0, OWN // BLK)
    def _(b):
        rows = pl.ds(pl.multiple_of(b * BLK, BLK), BLK)
        n2, inv2 = norm_parts(after(rows), DD)
        g = cot[rows, :].astype(F32) + norm_back(acc[rows, :], n2, inv2, gain_two, DD)
        low = g.astype(BF16)
        gmid[rows, :] = low
        gm = nt(low, dproj[...]).astype(BF16)
        prod = gm.astype(F32) * mixd[rows, :]
        for h in range(DH):
            lanes = slice(h * DHD, (h + 1) * DHD)
            gmix[h, rows, :] = gm[:, lanes]
            cen[h, rows, :] = jnp.sum(prod[:, lanes], axis=-1, keepdims=True)

    vis_x = nn(vis_pick, xall[...])
    exs[:, 3 * DI:] = nn(own_pick, gmid[...]).astype(BF16)
    for h in range(DH):
        lanes = slice(h * DHD, (h + 1) * DHD)
        k_vis = nn(vis_pick, kd[h]).astype(BF16)
        v_vis = nn(vis_pick, vd[h]).astype(BF16)
        p = jnp.exp(nt(qd[h], k_vis) - mxs[h]) * lis[h]
        ds = (p * (nt(gmix[h], v_vis) - cen[h])).astype(BF16)
        exs[:, DI + h * DHD:DI + (h + 1) * DHD] = tn(ds, qd[h]).astype(BF16)
        exs[:, 2 * DI + h * DHD:2 * DI + (h + 1) * DHD] = tn(p.astype(BF16), gmix[h]).astype(BF16)
        q_vis = nn(own_pick, qd[h]).astype(BF16)
        g_vis = nn(own_pick, gmix[h]).astype(BF16)
        s = nt(q_vis, kd[h])
        e = jnp.exp(s - jnp.max(s, axis=-1, keepdims=True))
        p = e * (1.0 / jnp.sum(e, axis=-1, keepdims=True))
        g = nt(g_vis, vd[h])
        c = jnp.sum(p * g, axis=-1, keepdims=True)
        ds = (p * (g - c)).astype(BF16)
        exs[:, lanes] = (nn(ds, kd[h]) * DEC_SCALE).astype(BF16)

    swap = exchange(exs, exr, 2)
    swap.start()
    swap.wait()
    both = exs[...].astype(F32) + exr[...].astype(F32)
    gattn = nt(both[:, 0:3 * DI].astype(BF16), dqkv[...])
    n1, inv1 = norm_parts(vis_x, DD)
    gstart = both[:, 3 * DI:] + norm_back(gattn, n1, inv1, gain_one, DD)
    real = lax.broadcasted_iota(jnp.int32, (ROWS, DD), 0) < VIS
    glow = jnp.where(real, gstart, 0.0).astype(BF16)

    genc_rows = nt(glow, down[...])
    gel = genc_rows.astype(BF16)
    gel_o[...] = gel
    xfull[...] = genc_rows
    gmx = nt(gel, proj[...]).astype(BF16)
    for h in range(HEADS):
        lanes = slice(h * HD, (h + 1) * HD)
        p = enc_probs(h)
        gm = gmx[:, lanes]
        g = nt(gm, vs[:, lanes])
        c = jnp.sum(p * g, axis=-1, keepdims=True)
        ds = (p * (g - c)).astype(BF16)
        gqkv_o[:, h * HD:(h + 1) * HD] = (nn(ds, ks[:, lanes]) * ENC_SCALE).astype(BF16)
        gqkv_o[:, HALF + h * HD:HALF + (h + 1) * HD] = tn(ds, qs[:, lanes]).astype(BF16)
        gqkv_o[:, 2 * HALF + h * HD:2 * HALF + (h + 1) * HD] = tn(p.astype(BF16), gm).astype(BF16)
    terms = nn(gqkv_o[...], wt[...]).astype(BF16)
    scaled = terms.astype(F32) * gain_enc
    mine = tokpad[...].astype(F32)
    theirs = tokrecv[...].astype(F32)
    full = jnp.concatenate([jnp.where(first, mine, theirs), jnp.where(first, theirs, mine)], axis=1)
    normed, inv = norm_parts(full, D)
    s1 = jnp.sum(scaled, axis=-1, keepdims=True)
    s2 = jnp.sum(scaled * normed, axis=-1, keepdims=True)
    sts[...] = jnp.where(lax.broadcasted_iota(jnp.int32, (ROWS, 128), 1) == 0, s1, s2)
    hts[...] = jnp.where(first, terms[:, HALF:], terms[:, 0:HALF])
    swap_a = exchange(hts, htr, 3)
    swap_b = exchange(sts, strr, 4)
    swap_a.start()
    swap_b.start()
    swap_a.wait()
    swap_b.wait()
    stats = sts[...] + strr[...]
    m1 = stats[:, 0:1] * (1.0 / D)
    m2 = stats[:, 1:2] * (1.0 / D)
    gh = jnp.where(first, terms[:, 0:HALF], terms[:, HALF:]).astype(F32) + htr[...].astype(F32)
    gain_mine = jnp.where(first, gain_enc[:, 0:HALF], gain_enc[:, HALF:])
    normed_mine = jnp.where(first, normed[:, 0:HALF], normed[:, HALF:])
    base = jnp.where(first, xfull[:, 0:HALF], xfull[:, HALF:D])
    out = base + inv * (gh * gain_mine - m1 - normed_mine * m2)
    gtok[...] = out[0:VIS, :]


def run_main(tok, visr, visc, rank, genc, maskt, gain1, gain2, wt, proj, down, dqkv, dproj, fc1, fc2, cot, pos):
    vm = pl.BlockSpec(memory_space=pltpu.VMEM)
    hbm = pl.BlockSpec(memory_space=pl.ANY)
    V = pltpu.VMEM
    big = (wt, proj, down, dqkv, dproj, fc1, fc2, cot, pos)
    scratch = [V(a.shape, a.dtype) for a in big] + [
        V((ROWS, HALF), BF16), V((ROWS, HALF), BF16), V((ROWS, D), F32), V((ROWS, 1), F32),
        V((ROWS, HALF), BF16), V((ROWS, HALF), BF16), V((ROWS, HALF), BF16),
        V((ROWS, DD), F32), V((ROWS, DD), F32),
        V((TUBES, DD), BF16), V((DH, TUBES, DHD), BF16), V((DH, TUBES, DHD), BF16),
        V((OWN, DD), F32), V((DH, OWN, DHD), BF16), V((OWN, DI), F32),
        V((DH, OWN, 1), F32), V((DH, OWN, 1), F32),
        V((OWN, DD), BF16), V((OWN, DD), F32), V((OWN, DD), BF16),
        V((DH, OWN, DHD), BF16), V((DH, OWN, 1), F32),
        V((ROWS, 3 * DI + DD), BF16), V((ROWS, 3 * DI + DD), BF16),
        V((ROWS, HALF), BF16), V((ROWS, HALF), BF16), V((ROWS, 128), F32), V((ROWS, 128), F32),
        pltpu.SemaphoreType.DMA((9,)), pltpu.SemaphoreType.DMA((5,)), pltpu.SemaphoreType.DMA((5,)),
    ]
    return pl.pallas_call(
        main_kernel,
        out_shape=(
            jax.ShapeDtypeStruct((VIS, HALF), F32),
            jax.ShapeDtypeStruct((ROWS, D), BF16),
            jax.ShapeDtypeStruct((ROWS, 3 * HALF), BF16),
            jax.ShapeDtypeStruct((ROWS, HALF), BF16),
            jax.ShapeDtypeStruct((ROWS, D), BF16),
        ),
        in_specs=[vm] * 8 + [hbm] * 9,
        out_specs=[vm] * 5,
        scratch_shapes=scratch,
        compiler_params=pltpu.CompilerParams(
            collective_id=0, has_side_effects=True, vmem_limit_bytes=60 * 1024 * 1024
        ),
    )(tok, visr, visc, rank, genc, maskt, gain1, gain2, *big)


PADW = 1536
QB = 528
PB = 176
TILE = 384


def weight_kernel(hid, gel, rq, rp, oq, op, hidg, gelg, rqg, rpg, ca, cb, ra, rb, sa, sb, ta, tb, fa, fb, ga, gb,
                  s1, r1, s2a, r2a, s2b, r2b, s3, r3, s4, r4):
    dp = lax.axis_index("dp")
    core = lax.axis_index("fsdp")
    z = dp // 16
    y = (dp // 4) % 4
    x = dp % 4

    def at_x(i):
        return (z * 16 + y * 4 + i, core)

    def at_y(i):
        return (z * 16 + i * 4 + x, core)

    def at_z(i):
        return (i * 16 + y * 4 + x, core)

    barrier = pltpu.get_barrier_semaphore()
    for d in range(1, 4):
        for place in (at_x((x + d) % 4), at_y((y + d) % 4), at_z((z + d) % 4)):
            pl.semaphore_signal(barrier, inc=1, device_id=place, device_id_type=MESH)
    pl.semaphore_wait(barrier, 9)

    def send(src, dst, ssem, rsem, place):
        copy = pltpu.make_async_remote_copy(
            src_ref=src, dst_ref=dst, send_sem=ssem, recv_sem=rsem, device_id=place, device_id_type=MESH
        )
        copy.start()
        return copy

    first = []
    for d in range(1, 4):
        to = (x + d) % 4
        place = at_x(to)
        first.append(send(hid, hidg.at[d], s1.at[0, d - 1], r1.at[0, d - 1], place))
        first.append(send(rq.at[to], rqg.at[d], s1.at[1, d - 1], r1.at[1, d - 1], place))
        first.append(send(gel, gelg.at[d], s1.at[2, d - 1], r1.at[2, d - 1], place))
        first.append(send(rp.at[to], rpg.at[d], s1.at[3, d - 1], r1.at[3, d - 1], place))
    hidg[0] = hid[...]
    gelg[0] = gel[...]
    rqg[0] = rq[x]
    rpg[0] = rp[x]
    for copy in first:
        copy.wait()

    second = []
    for d in (1, 2, 3, 0):
        zi = (z + d) % 4
        lanes = pl.ds(pl.multiple_of(zi * TILE, TILE), TILE)
        left = hidg[:, :, lanes].reshape(4 * ROWS, TILE)
        prod = tn(left, rqg[...].reshape(4 * ROWS, QB)).astype(BF16).reshape(4, 96, QB)
        ca[zi] = prod[:, :, 0:TILE]
        cb[zi, :, :, 0:QB - TILE] = prod[:, :, TILE:QB]
        left = gelg[:, :, lanes].reshape(4 * ROWS, TILE)
        prod = tn(left, rpg[...].reshape(4 * ROWS, PB)).astype(BF16).reshape(4, 96, PB)
        cb[zi, :, :, QB - TILE:QB - TILE + PB] = prod
        cb[zi, :, :, QB - TILE + PB:TILE] = jnp.zeros((4, 96, 2 * TILE - QB - PB), BF16)
        if d:
            second.append(send(ca.at[zi], ra.at[d - 1], s2a.at[d - 1], r2a.at[d - 1], at_z(zi)))
        for e in range(1, 4):
            yi = (y + e) % 4
            second.append(send(cb.at[zi, yi], rb.at[e - 1, zi], s2b.at[e - 1, d], r2b.at[e - 1, d], at_y(yi)))
    for copy in second:
        copy.wait()

    def total(own, got):
        return ((own.astype(F32) + got[0].astype(F32)) + (got[1].astype(F32) + got[2].astype(F32)))

    sa[...] = total(ca[z], ra).astype(BF16)
    sb[...] = total(cb[:, y], rb).astype(BF16)
    third = []
    for d in range(1, 4):
        yi = (y + d) % 4
        zi = (z + d) % 4
        third.append(send(sa.at[yi], ta.at[d - 1], s3.at[0, d - 1], r3.at[0, d - 1], at_y(yi)))
        third.append(send(sb.at[zi], tb.at[d - 1], s3.at[1, d - 1], r3.at[1, d - 1], at_z(zi)))
    for copy in third:
        copy.wait()
    fa[...] = total(sa[y], ta).reshape(4, 24, TILE)
    fb[...] = total(sb[z], tb).reshape(4, 24, TILE)
    fourth = []
    for d in range(1, 4):
        xi = (x + d) % 4
        fourth.append(send(fa.at[xi], ga.at[x], s4.at[0, d - 1], r4.at[0, d - 1], at_x(xi)))
        fourth.append(send(fb.at[xi], gb.at[x], s4.at[1, d - 1], r4.at[1, d - 1], at_x(xi)))
    ga[x] = fa[x]
    gb[x] = fb[x]
    for copy in fourth:
        copy.wait()
    for i in range(4):
        a = ga[i][0:22, :]
        b = gb[i][0:22, :]
        for j in range(6):
            head = 6 * i + j
            lo = HD * j
            hi = lo + HD
            if hi <= TILE:
                piece = a[:, lo:hi]
            elif lo >= TILE:
                piece = b[:, lo - TILE:hi - TILE]
            else:
                piece = jnp.concatenate([a[:, lo:TILE], b[:, 0:hi - TILE]], axis=1)
            oq[head // 8, :, (head % 8) * HD:(head % 8) * HD + HD] = piece
        op[:, PB * i:PB * i + PB] = b[:, QB - TILE:QB - TILE + PB]


def run_weight(hid, gel, rq, rp):
    vm = pl.BlockSpec(memory_space=pltpu.VMEM)
    V = pltpu.VMEM
    S = pltpu.SemaphoreType.DMA
    return pl.pallas_call(
        weight_kernel,
        out_shape=(jax.ShapeDtypeStruct((3, 22, HALF), F32), jax.ShapeDtypeStruct((22, HALF), F32)),
        in_specs=[vm] * 4,
        out_specs=(vm, vm),
        scratch_shapes=[
            V((4, ROWS, PADW), BF16), V((4, ROWS, PADW), BF16), V((4, ROWS, QB), BF16), V((4, ROWS, PB), BF16),
            V((4, 4, 96, TILE), BF16), V((4, 4, 96, TILE), BF16),
            V((3, 4, 96, TILE), BF16), V((3, 4, 96, TILE), BF16),
            V((4, 96, TILE), BF16), V((4, 96, TILE), BF16), V((3, 96, TILE), BF16), V((3, 96, TILE), BF16),
            V((4, 24, TILE), F32), V((4, 24, TILE), F32), V((4, 24, TILE), F32), V((4, 24, TILE), F32),
            S((4, 3)), S((4, 3)), S((3,)), S((3,)), S((3, 4)), S((3, 4)), S((2, 3)), S((2, 3)), S((2, 3)), S((2, 3)),
        ],
        compiler_params=pltpu.CompilerParams(
            collective_id=1, has_side_effects=True, vmem_limit_bytes=60 * 1024 * 1024
        ),
    )(hid, gel, rq, rp)


def spread_table():
    table = np.zeros((D, PADW), np.float32)
    cols = np.arange(D)
    table[cols, (cols // 22) * 24 + cols % 22] = 1.0
    return table


def per_device(
    tokens, vis_index, owner, enc_gain, enc_qkv, enc_proj, to_decoder, mask_token, dec_gain1,
    dec_qkv, dec_proj, dec_gain2, dec_fc1, dec_fc2, cotangent,
):
    me = lax.axis_index("fsdp")
    mine = (owner == me).astype(jnp.int32)
    rank = jnp.where(mine == 1, jnp.cumsum(mine, axis=1) - 1, -1)
    vis = jnp.pad(vis_index, ((0, 0), (0, ROWS - VIS)), constant_values=-1)
    wt = jnp.transpose(enc_qkv, (1, 2, 0)).reshape(3 * HALF, D)
    gtok, hidden, gqkv, mixed, gel = run_main(
        tokens[0], vis, vis.reshape(ROWS, 1), rank, enc_gain[None], mask_token[None],
        dec_gain1[None], dec_gain2[None], wt, enc_proj, to_decoder, dec_qkv, dec_proj,
        dec_fc1, dec_fc2, cotangent[0], jnp.asarray(position_rows()),
    )
    spread = jnp.asarray(spread_table(), BF16)
    hid_pad = jnp.dot(hidden, spread)
    gel_pad = jnp.dot(gel, spread)
    rq = jnp.transpose(gqkv.reshape(ROWS, 4, QB), (1, 0, 2))
    rp = jnp.transpose(mixed.reshape(ROWS, 4, PB), (1, 0, 2))
    gq, gp = run_weight(hid_pad, gel_pad, rq, rp)
    return gtok[None], jnp.transpose(gq, (1, 0, 2)), jnp.transpose(gp)


def solution(mesh):
    return jax.shard_map(
        per_device,
        mesh=mesh,
        in_specs=(
            P("dp", None, "fsdp"),
            P("dp", None),
            P("dp", None),
            P(),
            P(None, None, "fsdp"),
            P("fsdp", None),
            P(),
            P(),
            P(),
            P(),
            P(),
            P(),
            P(),
            P(),
            P("dp", "fsdp", None),
        ),
        out_specs=(P("dp", None, "fsdp"), P("dp", None, "fsdp"), P("fsdp", "dp")),
        check_vma=False,
    )
```

```python
import functools
import math

import jax
import jax.numpy as jnp
import numpy as np
from jax import lax
from jax.experimental import pallas as pl
from jax.experimental.pallas import tpu as pltpu
from jax.sharding import PartitionSpec as P

D = 1408
HALF = 704
HD = 88
HEADS = 8
DD = 512
DHD = 64
DH = 4
DI = 256
DF = 2048
TUBES = 1568
VIS = 157
ROWS = 160
OWN = 784
OWNP = 800
QROWS = 160
PADW = 1536
ZB = 384
QB = 528
QA = 256
PA = 384
HP = 176
EPS = 1e-06
ENC_SCALE = HD ** (-0.5)
DEC_SCALE = DHD ** (-0.5)
SQRT_HALF = 0.7071067811865476
INV_SQRT_TWO_PI = 0.3989422804014327
F32 = jnp.float32
BF16 = jnp.bfloat16
MESH = pl.DeviceIdType.MESH
SPREAD_FROM = (0, 256, 640, 1024)


def nn(a, b):
    return lax.dot_general(a, b, (((1,), (0,)), ((), ())), preferred_element_type=F32)


def nt(a, b):
    return lax.dot_general(a, b, (((1,), (1,)), ((), ())), preferred_element_type=F32)


def tn(a, b):
    return lax.dot_general(a, b, (((0,), (0,)), ((), ())), preferred_element_type=F32)


def norm_parts(values, width):
    mean = jnp.sum(values, axis=-1, keepdims=True) * (1.0 / width)
    centred = values - mean
    inv = lax.rsqrt(jnp.sum(centred * centred, axis=-1, keepdims=True) * (1.0 / width) + EPS)
    return centred * inv, inv


def norm_back(grad, normed, inv, gain, width):
    scaled = grad * gain
    first = jnp.sum(scaled, axis=-1, keepdims=True) * (1.0 / width)
    second = jnp.sum(scaled * normed, axis=-1, keepdims=True) * (1.0 / width)
    return inv * (scaled - first - normed * second)


def gelu_slope(u):
    return 0.5 * (1.0 + lax.erf(u * SQRT_HALF)) + u * jnp.exp(-0.5 * u * u) * INV_SQRT_TWO_PI


def position_rows():
    rates = np.exp(np.arange(DD // 2, dtype=np.float32) * np.float32(-2.0 * math.log(10000.0) / DD))
    angles = np.arange(TUBES, dtype=np.float32)[:, None] * rates
    return np.stack([np.sin(angles), np.cos(angles)], axis=-1).reshape(TUBES, DD).astype(np.float32)


def main_kernel(
    tok, visr, own, genc, maskt, gain1, gain2,
    wt_h, proj_h, down_h, dqkv_h, dproj_h, fc1_h, fc2_h, cot_h, pos_h,
    gtok, oq, op,
    wt, proj, down, dqkv, dproj, fc1, fc2, cot, pos,
    tokpad, tokrecv, xfull, qs, ks, vs, gms, lows, lowr, rank, rtile, spread,
    xall, kd, vd, kva, xown, qd, qall, mixd, stat, mlp, norm2, inv2s, acc, gmid, gmix, gmall,
    exs, exr, hts, htr, sts, strr,
    hidg, mixg, gelp, gelg, rq, rqg,
    ca, cb, ra, rb, sa, sb, ta, tb, fa, fb, ga, gb,
    pa, pb, qra, qrb, qsa, qsb, qta, qtb,
    local, send, recv, sh, rh, sm, rm, sg, rg, sq, rqs,
    s2a, r2a, s2b, r2b, s3, r3, s4, r4, s5, r5, s6, r6,
):
    me = lax.axis_index("fsdp")
    dp = lax.axis_index("dp")
    z = dp // 16
    y = (dp // 4) % 4
    x = dp % 4
    other = 1 - me
    first = me == 0

    def at_x(i):
        return (z * 16 + y * 4 + i, me)

    def at_y(i):
        return (z * 16 + i * 4 + x, me)

    def at_z(i):
        return (i * 16 + y * 4 + x, me)

    loads = [
        pltpu.make_async_copy(src, dst, local.at[i])
        for i, (src, dst) in enumerate(
            [(wt_h, wt), (proj_h, proj), (down_h, down), (pos_h, pos), (dqkv_h, dqkv),
             (dproj_h, dproj), (fc1_h, fc1), (fc2_h, fc2), (cot_h, cot.at[0:OWN])]
        )
    ]
    l_wt, l_proj, l_down, l_pos, l_dqkv, l_dproj, l_fc1, l_fc2, l_cot = loads
    l_wt.start()
    l_proj.start()
    l_down.start()

    def push(src, dst, ssem, rsem, place):
        copy = pltpu.make_async_remote_copy(
            src_ref=src, dst_ref=dst, send_sem=ssem, recv_sem=rsem, device_id=place, device_id_type=MESH
        )
        copy.start()
        return copy

    def exchange(src, dst, i):
        return push(src, dst, send.at[i], recv.at[i], (dp, other))

    barrier = pltpu.get_barrier_semaphore()
    pl.semaphore_signal(barrier, inc=1, device_id=(dp, other), device_id_type=MESH)
    for d in range(1, 4):
        for place in (at_x((x + d) % 4), at_y((y + d) % 4), at_z((z + d) % 4)):
            pl.semaphore_signal(barrier, inc=1, device_id=place, device_id_type=MESH)

    cot[OWN:OWNP, :] = jnp.zeros((OWNP - OWN, DD), BF16)
    tokpad[...] = jnp.zeros((ROWS, HALF), BF16)
    tokpad[0:VIS, :] = tok[...]
    pl.semaphore_wait(barrier, 10)
    swap = exchange(tokpad, tokrecv, 0)

    mine_row = (own[...] == me).astype(F32)
    rtile[...] = jnp.zeros((16, 128), F32)
    for i in range(13):
        wide = min(128, TUBES - 128 * i)
        rtile[i:i + 1, 0:wide] = mine_row[:, 128 * i:128 * i + wide]
    tiles = rtile[...]
    upper = lax.broadcasted_iota(jnp.int32, (128, 128), 0) <= lax.broadcasted_iota(jnp.int32, (128, 128), 1)
    inside = nn(tiles.astype(BF16), upper.astype(F32).astype(BF16))
    lower = lax.broadcasted_iota(jnp.int32, (16, 16), 0) > lax.broadcasted_iota(jnp.int32, (16, 16), 1)
    before = nn(lower.astype(F32).astype(BF16), jnp.broadcast_to(inside[:, 127:128], (16, 128)).astype(BF16))
    rtile[...] = jnp.where(tiles > 0.0, inside + before, 0.0)
    for i in range(13):
        wide = min(128, TUBES - 128 * i)
        rank[:, 128 * i:128 * i + wide] = rtile[i:i + 1, 0:wide].astype(jnp.int32) - 1

    lane = lax.broadcasted_iota(jnp.int32, (1, ZB), 1)
    group = (lane.astype(F32) * (1.0 / 24.0) + 0.01).astype(jnp.int32)
    within = lane - group * 24
    for i in range(4):
        shift = 352 * i - SPREAD_FROM[i]
        want = jnp.where(within < 22, group * 22 + within + shift, -1)
        rows = lax.broadcasted_iota(jnp.int32, (512, ZB), 0)
        spread[i] = (rows == want).astype(F32).astype(BF16)

    def spread_cols(v):
        parts = []
        for i in range(4):
            lo = SPREAD_FROM[i]
            hi = min(lo + 512, D)
            parts.append(nn(v[:, lo:hi], spread[i, 0:hi - lo, :]).astype(BF16))
        return parts

    vis_row = visr[...]
    eye = lax.broadcasted_iota(jnp.int32, (ROWS, VIS), 0) == lax.broadcasted_iota(jnp.int32, (ROWS, VIS), 1)
    vis_col = jnp.sum(jnp.where(eye, vis_row + 1, 0), axis=1, keepdims=True) - 1
    vis_hit = lax.broadcasted_iota(jnp.int32, (ROWS, TUBES), 1) == vis_col
    vis_pick = vis_hit.astype(F32).astype(BF16)
    slot_of = jnp.sum(jnp.where(vis_hit, rank[...] + 1, 0), axis=1, keepdims=True) - 1
    own_pick = (lax.broadcasted_iota(jnp.int32, (ROWS, OWNP), 1) == slot_of).astype(F32).astype(BF16)

    swap.wait()
    gain_enc = genc[...].reshape(1, D).astype(F32)

    def all_tokens():
        mine = tokpad[...].astype(F32)
        theirs = tokrecv[...].astype(F32)
        xfull[:, 0:HALF] = jnp.where(first, mine, theirs)
        xfull[:, HALF:D] = jnp.where(first, theirs, mine)
        return xfull[...]

    normed, inv = norm_parts(all_tokens(), D)
    hidden = (normed * gain_enc).astype(BF16)
    for i, part in enumerate(spread_cols(hidden)):
        hidg[0, :, i * ZB:(i + 1) * ZB] = part
    hid_sends = [
        push(hidg.at[0], hidg.at[d], sh.at[d - 1], rh.at[d - 1], at_x((x + d) % 4)) for d in range(1, 4)
    ]
    l_wt.wait()
    l_pos.start()
    l_dqkv.start()
    q = (nt(hidden, wt[0:HALF, :]) * ENC_SCALE).astype(BF16)
    k = nt(hidden, wt[HALF:2 * HALF, :]).astype(BF16)
    v = nt(hidden, wt[2 * HALF:3 * HALF, :]).astype(BF16)
    for h in range(HEADS):
        lanes = slice(h * HD, (h + 1) * HD)
        qs[h] = q[:, lanes]
        ks[h] = k[:, lanes]
        vs[h] = v[:, lanes]
    key_ok = lax.broadcasted_iota(jnp.int32, (ROWS, ROWS), 1) < VIS

    def enc_probs(h):
        s = jnp.where(key_ok, nt(qs[h], ks[h]), -1e30)
        e = jnp.exp(s - jnp.max(s, axis=-1, keepdims=True))
        return e * (1.0 / jnp.sum(e, axis=-1, keepdims=True))

    for h in range(HEADS):
        mixg[0, :, h * HD:(h + 1) * HD] = nn(enc_probs(h).astype(BF16), vs[h]).astype(BF16)
    mix_sends = [
        push(mixg.at[0], mixg.at[d], sm.at[d - 1], rm.at[d - 1], at_z((z + d) % 4)) for d in range(1, 4)
    ]
    l_proj.wait()
    heads_term = nn(mixg[0], proj[...])
    part_enc = (jnp.where(first, xfull[...], 0.0) + heads_term).astype(BF16)
    l_down.wait()
    lows[...] = nn(part_enc, down[...])
    swap = exchange(lows, lowr, 1)
    l_dproj.start()
    l_fc1.start()
    l_fc2.start()
    l_cot.start()

    swap.wait()
    lowered = (lows[...] + lowr[...]).astype(BF16)
    l_pos.wait()
    l_dqkv.wait()
    gain_one = gain1[...].reshape(1, DD).astype(F32)
    gain_two = gain2[...].reshape(1, DD).astype(F32)
    mask_row = maskt[...].reshape(1, DD).astype(F32)

    vd[...] = jnp.zeros((DH, TUBES, 128), BF16)
    vd[:, :, DHD:DHD + 1] = jnp.ones((DH, TUBES, 1), BF16)

    @pl.loop(0, 2)
    def _(b):
        rows = pl.ds(pl.multiple_of(b * OWN, 16), OWN)
        hit = lax.broadcasted_iota(jnp.int32, (OWN, VIS), 0) + b * OWN == vis_row
        hit = hit.astype(F32)
        placed = nn(hit.astype(BF16), lowered[0:VIS])
        covered = jnp.sum(hit, axis=1, keepdims=True)
        start = (placed + (1.0 - covered) * mask_row + pos[rows, :]).astype(BF16)
        xall[rows, :] = start
        n1, _ = norm_parts(start.astype(F32), DD)
        attn_in = (n1 * gain_one).astype(BF16)
        kv = nn(attn_in, dqkv[:, DI:3 * DI]).astype(BF16)
        kva[rows, :] = kv
        for h in range(DH):
            kd[h, rows, :] = kv[:, h * DHD:(h + 1) * DHD]
            vd[h, rows, 0:DHD] = kv[:, DI + h * DHD:DI + (h + 1) * DHD]

    for lo in (0, 400):
        rows = slice(lo, lo + 400)
        pick = lax.broadcasted_iota(jnp.int32, (400, TUBES), 0) + lo == rank[...]
        start = nn(pick.astype(F32).astype(BF16), xall[...])
        xown[rows, :] = start.astype(BF16)
        n1, _ = norm_parts(start, DD)
        attn_in = (n1 * gain_one).astype(BF16)
        q = (nn(attn_in, dqkv[:, 0:DI]) * DEC_SCALE).astype(BF16)
        qall[rows, :] = q
        for h in range(DH):
            qd[h, rows, :] = q[:, h * DHD:(h + 1) * DHD]

    @pl.loop(0, OWNP // QROWS)
    def _(b):
        rows = pl.ds(pl.multiple_of(b * QROWS, QROWS), QROWS)
        scores = [nt(qd[h, rows, :], kd[h]) for h in range(2)]
        for h in range(DH):
            s = scores[h]
            top = jnp.max(s, axis=-1, keepdims=True)
            if h + 2 < DH:
                scores.append(nt(qd[h + 2, rows, :], kd[h + 2]))
            e = jnp.exp(s - top).astype(BF16)
            o = nn(e, vd[h])
            total = 1.0 / o[:, DHD:DHD + 1]
            stat[rows, h:h + 1] = top
            stat[rows, 4 + h:5 + h] = total
            mixd[rows, h * DHD:(h + 1) * DHD] = o[:, 0:DHD] * total

    l_dproj.wait()

    for lo, hi in ((0, 400), (400, OWNP)):
        after = (xown[lo:hi, :].astype(F32) + nn(mixd[lo:hi, :].astype(BF16), dproj[...])).astype(BF16).astype(F32)
        n2, inv2 = norm_parts(after, DD)
        norm2[lo:hi, :] = n2
        inv2s[lo:hi, :] = inv2
        mlp[lo:hi, :] = (n2 * gain_two).astype(BF16)

    l_fc1.wait()
    l_fc2.wait()
    l_cot.wait()
    held = None
    for c in range(DF // 512):
        part = slice(c * 512, (c + 1) * 512)
        up = nn(mlp[...], fc1[:, part])
        gact = nt(cot[...], fc2[part, :])
        if c == 1:
            acc[...] = nt(held, fc1[:, 0:512])
        elif c > 1:
            acc[...] += nt(held, fc1[:, (c - 1) * 512:c * 512])
        held = (gact * gelu_slope(up)).astype(BF16)
    acc[...] += nt(held, fc1[:, DF - 512:DF])

    for lo, hi in ((0, 400), (400, OWNP)):
        g = cot[lo:hi, :].astype(F32) + norm_back(acc[lo:hi, :], norm2[lo:hi, :], inv2s[lo:hi, :], gain_two, DD)
        low = g.astype(BF16)
        gmid[lo:hi, :] = low
        gm = nt(low, dproj[...]).astype(BF16)
        gmall[lo:hi, :] = gm
        prod = gm.astype(F32) * mixd[lo:hi, :]
        for h in range(DH):
            lanes = slice(h * DHD, (h + 1) * DHD)
            gmix[h, lo:hi, :] = gm[:, lanes]
            stat[lo:hi, 8 + h:9 + h] = jnp.sum(prod[:, lanes], axis=-1, keepdims=True)

    vis_x = nn(vis_pick, xall[...])
    vis_kv = nn(vis_pick, kva[...]).astype(BF16)
    vis_q = nn(own_pick, qall[...]).astype(BF16)
    vis_g = nn(own_pick, gmall[...]).astype(BF16)
    exs[:, 3 * DI:] = nn(own_pick, gmid[...]).astype(BF16)
    for h in range(DH):
        lanes = slice(h * DHD, (h + 1) * DHD)
        k_vis = vis_kv[:, lanes]
        v_vis = vis_kv[:, DI + h * DHD:DI + (h + 1) * DHD]
        p = jnp.exp(nt(qd[h], k_vis) - stat[:, h:h + 1]) * stat[:, 4 + h:5 + h]
        ds = (p * (nt(gmix[h], v_vis) - stat[:, 8 + h:9 + h])).astype(BF16)
        exs[:, DI + h * DHD:DI + (h + 1) * DHD] = tn(ds, qd[h]).astype(BF16)
        exs[:, 2 * DI + h * DHD:2 * DI + (h + 1) * DHD] = tn(p.astype(BF16), gmix[h]).astype(BF16)
        s = nt(vis_q[:, lanes], kd[h])
        e = jnp.exp(s - jnp.max(s, axis=-1, keepdims=True))
        p = e * (1.0 / jnp.sum(e, axis=-1, keepdims=True))
        g = nt(vis_g[:, lanes], vd[h, :, 0:DHD])
        c = jnp.sum(p * g, axis=-1, keepdims=True)
        ds = (p * (g - c)).astype(BF16)
        exs[:, lanes] = (nn(ds, kd[h]) * DEC_SCALE).astype(BF16)

    swap = exchange(exs, exr, 2)
    swap.wait()
    both = exs[...].astype(F32) + exr[...].astype(F32)
    gattn = nt(both[:, 0:3 * DI].astype(BF16), dqkv[...])
    n1, inv1 = norm_parts(vis_x, DD)
    gstart = both[:, 3 * DI:] + norm_back(gattn, n1, inv1, gain_one, DD)
    real = lax.broadcasted_iota(jnp.int32, (ROWS, DD), 0) < VIS
    glow = jnp.where(real, gstart, 0.0).astype(BF16)

    genc_rows = nt(glow, down[...])
    gel = genc_rows.astype(BF16)
    for i, part in enumerate(spread_cols(gel)):
        gelp[i] = part
    gel_sends = []
    for d in range(1, 4):
        zi = (z + d) % 4
        gel_sends.append(push(gelp.at[zi], gelg.at[d], sg.at[d - 1], rg.at[d - 1], at_z(zi)))
    gelg[0] = gelp[z]
    gmx = nt(gel, proj[...]).astype(BF16)
    for h in range(HEADS):
        gms[h] = gmx[:, h * HD:(h + 1) * HD]
    rq_sends = []
    for d in (1, 2, 3, 0):
        j = (x + d) % 4
        for i in range(2):
            h = 2 * j + i
            p = enc_probs(h)
            gm = gms[h]
            g = nt(gm, vs[h])
            c = jnp.sum(p * g, axis=-1, keepdims=True)
            ds = (p * (g - c)).astype(BF16)
            rq[j, :, i * HD:(i + 1) * HD] = (nn(ds, ks[h]) * ENC_SCALE).astype(BF16)
            rq[j, :, HP + i * HD:HP + (i + 1) * HD] = tn(ds, qs[h]).astype(BF16)
            rq[j, :, 2 * HP + i * HD:2 * HP + (i + 1) * HD] = tn(p.astype(BF16), gm).astype(BF16)
        if d:
            rq_sends.append(push(rq.at[j], rqg.at[d], sq.at[d - 1], rqs.at[d - 1], at_x(j)))
        else:
            rqg[0] = rq[j]

    def total(mine, got):
        return (mine.astype(F32) + got[0].astype(F32)) + (got[1].astype(F32) + got[2].astype(F32))

    for copy in gel_sends:
        copy.wait()
    for copy in mix_sends:
        copy.wait()
    prod = tn(gelg[...].reshape(4 * ROWS, ZB), mixg[...].reshape(4 * ROWS, HALF)).astype(BF16).reshape(4, 4, 24, HALF)
    pa[...] = prod[:, :, :, 0:PA].reshape(4, 96, PA)
    for i in range(4):
        pb[i, :, :, 0:HALF - PA] = prod[:, i, :, PA:HALF]
        pb[i, :, :, HALF - PA:PA] = jnp.zeros((4, 24, 2 * PA - HALF), BF16)
    p_sends = []
    for d in range(1, 4):
        yi = (y + d) % 4
        xi = (x + d) % 4
        p_sends.append(push(pa.at[yi], qra.at[d - 1], s5.at[0, d - 1], r5.at[0, d - 1], at_y(yi)))
        p_sends.append(push(pb.at[xi], qrb.at[d - 1], s5.at[1, d - 1], r5.at[1, d - 1], at_x(xi)))

    terms = jnp.zeros((ROWS, D), F32)
    for j in range(4):
        for part in range(3):
            terms += nn(rq[j, :, part * HP:(part + 1) * HP], wt[part * HALF + j * HP:part * HALF + (j + 1) * HP, :])
    terms = terms.astype(BF16)
    scaled = terms.astype(F32) * gain_enc
    normed, inv = norm_parts(all_tokens(), D)
    s1 = jnp.sum(scaled, axis=-1, keepdims=True)
    s2 = jnp.sum(scaled * normed, axis=-1, keepdims=True)
    sts[...] = jnp.where(lax.broadcasted_iota(jnp.int32, (ROWS, 128), 1) == 0, s1, s2)
    hts[...] = jnp.where(first, terms[:, HALF:], terms[:, 0:HALF])
    swap_a = exchange(hts, htr, 3)
    swap_b = exchange(sts, strr, 4)

    for copy in hid_sends:
        copy.wait()
    for copy in rq_sends:
        copy.wait()
    second = []
    for d in (1, 2, 3, 0):
        zi = (z + d) % 4
        lanes = pl.ds(pl.multiple_of(zi * ZB, ZB), ZB)
        left = hidg[:, :, lanes].reshape(4 * ROWS, ZB)
        prod = tn(left, rqg[...].reshape(4 * ROWS, QB)).astype(BF16).reshape(4, 96, QB)
        ca[zi] = prod[:, :, 0:QA]
        cb[zi] = prod[:, :, QA:QB]
        if d:
            second.append(push(ca.at[zi], ra.at[d - 1], s2a.at[d - 1], r2a.at[d - 1], at_z(zi)))
        for e in range(1, 4):
            yi = (y + e) % 4
            second.append(push(cb.at[zi, yi], rb.at[e - 1, zi], s2b.at[e - 1, d], r2b.at[e - 1, d], at_y(yi)))

    swap_a.wait()
    swap_b.wait()
    stats = sts[...] + strr[...]
    m1 = stats[:, 0:1] * (1.0 / D)
    m2 = stats[:, 1:2] * (1.0 / D)
    gh = jnp.where(first, terms[:, 0:HALF], terms[:, HALF:]).astype(F32) + htr[...].astype(F32)
    gain_mine = jnp.where(first, gain_enc[:, 0:HALF], gain_enc[:, HALF:])
    normed_mine = jnp.where(first, normed[:, 0:HALF], normed[:, HALF:])
    base = jnp.where(first, genc_rows[:, 0:HALF], genc_rows[:, HALF:D])
    out = base + inv * (gh * gain_mine - m1 - normed_mine * m2)
    gtok[...] = out[0:VIS, :]

    for copy in p_sends:
        copy.wait()
    qsa[...] = total(pa[y], qra).astype(BF16).reshape(4, 24, PA)
    qsb[...] = total(pb[x], qrb).astype(BF16)
    p_sends = []
    for d in range(1, 4):
        yi = (y + d) % 4
        xi = (x + d) % 4
        p_sends.append(push(qsa.at[xi], qta.at[d - 1], s6.at[0, d - 1], r6.at[0, d - 1], at_x(xi)))
        p_sends.append(push(qsb.at[yi], qtb.at[d - 1], s6.at[1, d - 1], r6.at[1, d - 1], at_y(yi)))

    for copy in second:
        copy.wait()
    sa[...] = total(ca[z], ra).astype(BF16)
    sb[...] = total(cb[:, y], rb).astype(BF16)
    third = []
    for d in range(1, 4):
        yi = (y + d) % 4
        zi = (z + d) % 4
        third.append(push(sa.at[yi], ta.at[d - 1], s3.at[0, d - 1], r3.at[0, d - 1], at_y(yi)))
        third.append(push(sb.at[zi], tb.at[d - 1], s3.at[1, d - 1], r3.at[1, d - 1], at_z(zi)))
    for copy in p_sends:
        copy.wait()
    op[:, 0:PA] = total(qsa[x], qta)[0:22, :]
    op[:, PA:HALF] = total(qsb[y], qtb)[0:22, 0:HALF - PA]
    for copy in third:
        copy.wait()
    fa[...] = total(sa[y], ta).reshape(4, 24, QA)
    fb[...] = total(sb[z], tb).reshape(4, 24, QB - QA)
    fourth = []
    for d in range(1, 4):
        xi = (x + d) % 4
        fourth.append(push(fa.at[xi], ga.at[x], s4.at[0, d - 1], r4.at[0, d - 1], at_x(xi)))
        fourth.append(push(fb.at[xi], gb.at[x], s4.at[1, d - 1], r4.at[1, d - 1], at_x(xi)))
    ga[x] = fa[x]
    gb[x] = fb[x]
    for copy in fourth:
        copy.wait()
    for i in range(4):
        a = ga[i]
        b = gb[i]
        cols = slice(HP * i, HP * (i + 1))
        oq[0, :, cols] = a[0:22, 0:HP]
        oq[1, :, HP * i:HP * i + QA - HP] = a[0:22, HP:QA]
        oq[1, :, HP * i + QA - HP:HP * (i + 1)] = b[0:22, 0:2 * HP - QA]
        oq[2, :, cols] = b[0:22, 2 * HP - QA:QB - QA]


def run_main(tok, visr, own, genc, maskt, gain1, gain2, wt, proj, down, dqkv, dproj, fc1, fc2, cot, pos):
    vm = pl.BlockSpec(memory_space=pltpu.VMEM)
    hbm = pl.BlockSpec(memory_space=pl.ANY)
    V = pltpu.VMEM
    S = pltpu.SemaphoreType.DMA
    big = (wt, proj, down, dqkv, dproj, fc1, fc2, cot, pos)
    half = (ROWS, HALF)
    scratch = [V(a.shape, a.dtype) for a in big[:7]] + [
        V((OWNP, DD), BF16), V((TUBES, DD), F32),
        V(half, BF16), V(half, BF16), V((ROWS, D), F32),
        V((HEADS, ROWS, HD), BF16), V((HEADS, ROWS, HD), BF16), V((HEADS, ROWS, HD), BF16),
        V((HEADS, ROWS, HD), BF16),
        V((ROWS, DD), F32), V((ROWS, DD), F32), V((1, TUBES), jnp.int32), V((16, 128), F32), V((4, 512, ZB), BF16),
        V((TUBES, DD), BF16), V((DH, TUBES, DHD), BF16), V((DH, TUBES, 128), BF16), V((TUBES, 2 * DI), BF16),
        V((OWNP, DD), BF16), V((DH, OWNP, DHD), BF16), V((OWNP, DI), BF16), V((OWNP, DI), F32),
        V((OWNP, 16), F32),
        V((OWNP, DD), BF16), V((OWNP, DD), F32), V((OWNP, 1), F32), V((OWNP, DD), F32), V((OWNP, DD), BF16),
        V((DH, OWNP, DHD), BF16), V((OWNP, DI), BF16),
        V((ROWS, 3 * DI + DD), BF16), V((ROWS, 3 * DI + DD), BF16),
        V(half, BF16), V(half, BF16), V((ROWS, 128), F32), V((ROWS, 128), F32),
        V((4, ROWS, PADW), BF16), V((4, ROWS, HALF), BF16), V((4, ROWS, ZB), BF16), V((4, ROWS, ZB), BF16),
        V((4, ROWS, QB), BF16), V((4, ROWS, QB), BF16),
        V((4, 4, 96, QA), BF16), V((4, 4, 96, QB - QA), BF16),
        V((3, 4, 96, QA), BF16), V((3, 4, 96, QB - QA), BF16),
        V((4, 96, QA), BF16), V((4, 96, QB - QA), BF16), V((3, 96, QA), BF16), V((3, 96, QB - QA), BF16),
        V((4, 24, QA), F32), V((4, 24, QB - QA), F32), V((4, 24, QA), F32), V((4, 24, QB - QA), F32),
        V((4, 96, PA), BF16), V((4, 4, 24, PA), BF16), V((3, 96, PA), BF16), V((3, 4, 24, PA), BF16),
        V((4, 24, PA), BF16), V((4, 24, PA), BF16), V((3, 24, PA), BF16), V((3, 24, PA), BF16),
        S((9,)), S((5,)), S((5,)), S((3,)), S((3,)), S((3,)), S((3,)), S((3,)), S((3,)), S((3,)), S((3,)),
        S((3,)), S((3,)), S((3, 4)), S((3, 4)), S((2, 3)), S((2, 3)), S((2, 3)), S((2, 3)),
        S((2, 3)), S((2, 3)), S((2, 3)), S((2, 3)),
    ]
    return pl.pallas_call(
        main_kernel,
        out_shape=(
            jax.ShapeDtypeStruct((VIS, HALF), F32),
            jax.ShapeDtypeStruct((3, 22, HALF), F32),
            jax.ShapeDtypeStruct((22, HALF), F32),
        ),
        in_specs=[vm] * 7 + [hbm] * 9,
        out_specs=[vm] * 3,
        scratch_shapes=scratch,
        compiler_params=pltpu.CompilerParams(
            collective_id=0, has_side_effects=True, vmem_limit_bytes=60 * 1024 * 1024
        ),
    )(tok, visr, own, genc, maskt, gain1, gain2, *big)


def per_device(
    tokens, vis_index, owner, enc_gain, enc_qkv, enc_proj, to_decoder, mask_token, dec_gain1,
    dec_qkv, dec_proj, dec_gain2, dec_fc1, dec_fc2, cotangent,
):
    wt = jnp.transpose(enc_qkv, (1, 2, 0)).reshape(3 * HALF, D)
    gtok, gq, gp = run_main(
        tokens[0], vis_index, owner, enc_gain, mask_token, dec_gain1, dec_gain2, wt, enc_proj,
        to_decoder, dec_qkv, dec_proj, dec_fc1, dec_fc2, cotangent[0], jnp.asarray(position_rows()),
    )
    return gtok[None], jnp.transpose(gq, (1, 0, 2)), jnp.transpose(gp)


def solution(mesh):
    return jax.shard_map(
        per_device,
        mesh=mesh,
        in_specs=(
            P("dp", None, "fsdp"),
            P("dp", None),
            P("dp", None),
            P(),
            P(None, None, "fsdp"),
            P("fsdp", None),
            P(),
            P(),
            P(),
            P(),
            P(),
            P(),
            P(),
            P(),
            P("dp", "fsdp", None),
        ),
        out_specs=(P("dp", None, "fsdp"), P("dp", None, "fsdp"), P("fsdp", "dp")),
        check_vma=False,
    )
```

```python
import functools
import math

import jax
import jax.numpy as jnp
import numpy as np
from jax import lax
from jax.experimental import pallas as pl
from jax.experimental.pallas import tpu as pltpu
from jax.sharding import PartitionSpec as P

D = 1408
HALF = 704
HD = 88
HEADS = 8
DD = 512
DHD = 64
DH = 4
DI = 256
DF = 2048
TUBES = 1568
VIS = 157
ROWS = 160
OWN = 784
OWNP = 800
QROWS = 160
PADW = 1536
ZB = 384
PA = 384
HP = 176
EPS = 1e-06
ENC_SCALE = HD ** (-0.5)
DEC_SCALE = DHD ** (-0.5)
SQRT_HALF = 0.7071067811865476
INV_SQRT_TWO_PI = 0.3989422804014327
F32 = jnp.float32
BF16 = jnp.bfloat16
MESH = pl.DeviceIdType.MESH
SPREAD_FROM = (0, 256, 640, 1024)
ROUTES = ((2, 1, 0), (1, 0, 2), (0, 2, 1))


def nn(a, b):
    return lax.dot_general(a, b, (((1,), (0,)), ((), ())), preferred_element_type=F32)


def nt(a, b):
    return lax.dot_general(a, b, (((1,), (1,)), ((), ())), preferred_element_type=F32)


def tn(a, b):
    return lax.dot_general(a, b, (((0,), (0,)), ((), ())), preferred_element_type=F32)


def norm_parts(values, width):
    mean = jnp.sum(values, axis=-1, keepdims=True) * (1.0 / width)
    centred = values - mean
    inv = lax.rsqrt(jnp.sum(centred * centred, axis=-1, keepdims=True) * (1.0 / width) + EPS)
    return centred * inv, inv


def norm_back(grad, normed, inv, gain, width):
    scaled = grad * gain
    first = jnp.sum(scaled, axis=-1, keepdims=True) * (1.0 / width)
    second = jnp.sum(scaled * normed, axis=-1, keepdims=True) * (1.0 / width)
    return inv * (scaled - first - normed * second)


def gelu_slope(u):
    return 0.5 * (1.0 + lax.erf(u * SQRT_HALF)) + u * jnp.exp(-0.5 * u * u) * INV_SQRT_TWO_PI


def position_rows():
    rates = np.exp(np.arange(DD // 2, dtype=np.float32) * np.float32(-2.0 * math.log(10000.0) / DD))
    angles = np.arange(TUBES, dtype=np.float32)[:, None] * rates
    return np.stack([np.sin(angles), np.cos(angles)], axis=-1).reshape(TUBES, DD).astype(np.float32)


def main_kernel(
    tok, visr, own, genc, maskt, gain1, gain2,
    wt_h, proj_h, down_h, dqkv_h, dproj_h, fc1_h, fc2_h, cot_h, pos_h,
    gtok, oq, op,
    wt, proj, down, dqkv, dproj, fc1, fc2, cot, pos,
    tokpad, tokrecv, xfull, qs, ks, vs, gms, lows, lowr, rank, rtile, spread,
    xall, kd, vd, kva, xown, qd, qall, mixd, stat, mlp, inv2s, gmid, gmix, gmall,
    exs, exr, hts, htr, sts, strr,
    hid, hidg, mixg, gelp, gelg, rq, gqkv, rqg,
    cs, ra, sa, ta, fa, ga,
    pa, pb, qra, qrb, qsa, qsb, qta, qtb,
    local, send, recv, sh, rh, sm, rm, sg, rg, sq, rqs,
    sx, rx, s3, r3, s4, r4, s5, r5, s6, r6,
):
    me = lax.axis_index("fsdp")
    dp = lax.axis_index("dp")
    z = dp // 16
    y = (dp // 4) % 4
    x = dp % 4
    other = 1 - me
    first = me == 0

    def at_x(i):
        return (z * 16 + y * 4 + i, me)

    def at_y(i):
        return (z * 16 + i * 4 + x, me)

    def at_z(i):
        return (i * 16 + y * 4 + x, me)

    place_on = (at_z, at_y, at_x)
    here = (z, y, x)

    def take(ref, axis, i):
        if axis == 0:
            return ref.at[i]
        return ref.at[:, i] if axis == 1 else ref.at[:, :, i]

    loads = [
        pltpu.make_async_copy(src, dst, local.at[i])
        for i, (src, dst) in enumerate(
            [(wt_h, wt), (proj_h, proj), (down_h, down), (pos_h, pos.at[0:TUBES]), (dqkv_h, dqkv),
             (dproj_h, dproj), (fc1_h, fc1), (fc2_h, fc2), (cot_h, cot.at[0:OWN])]
        )
    ]
    l_wt, l_proj, l_down, l_pos, l_dqkv, l_dproj, l_fc1, l_fc2, l_cot = loads
    l_wt.start()
    l_proj.start()
    l_down.start()

    def push(src, dst, ssem, rsem, place):
        copy = pltpu.make_async_remote_copy(
            src_ref=src, dst_ref=dst, send_sem=ssem, recv_sem=rsem, device_id=place, device_id_type=MESH
        )
        copy.start()
        return copy

    def exchange(src, dst, i):
        return push(src, dst, send.at[i], recv.at[i], (dp, other))

    barrier = pltpu.get_barrier_semaphore()
    pl.semaphore_signal(barrier, inc=1, device_id=(dp, other), device_id_type=MESH)
    for d in range(1, 4):
        for place in (at_x((x + d) % 4), at_y((y + d) % 4), at_z((z + d) % 4)):
            pl.semaphore_signal(barrier, inc=1, device_id=place, device_id_type=MESH)

    cot[OWN:OWNP, :] = jnp.zeros((OWNP - OWN, DD), BF16)
    tokpad[...] = jnp.zeros((ROWS, HALF), BF16)
    tokpad[0:VIS, :] = tok[...]
    pl.semaphore_wait(barrier, 10)
    swap = exchange(tokpad, tokrecv, 0)

    mine_row = (own[...] == me).astype(F32)
    rtile[...] = jnp.zeros((16, 128), F32)
    for i in range(13):
        wide = min(128, TUBES - 128 * i)
        rtile[i:i + 1, 0:wide] = mine_row[:, 128 * i:128 * i + wide]
    tiles = rtile[...]
    upper = lax.broadcasted_iota(jnp.int32, (128, 128), 0) <= lax.broadcasted_iota(jnp.int32, (128, 128), 1)
    inside = nn(tiles.astype(BF16), upper.astype(F32).astype(BF16))
    lower = lax.broadcasted_iota(jnp.int32, (16, 16), 0) > lax.broadcasted_iota(jnp.int32, (16, 16), 1)
    before = nn(lower.astype(F32).astype(BF16), jnp.broadcast_to(inside[:, 127:128], (16, 128)).astype(BF16))
    rtile[...] = jnp.where(tiles > 0.0, inside + before, 0.0)
    for i in range(13):
        wide = min(128, TUBES - 128 * i)
        rank[:, 128 * i:128 * i + wide] = rtile[i:i + 1, 0:wide].astype(jnp.int32) - 1

    lane = lax.broadcasted_iota(jnp.int32, (1, ZB), 1)
    group = (lane.astype(F32) * (1.0 / 24.0) + 0.01).astype(jnp.int32)
    within = lane - group * 24
    for i in range(4):
        shift = 352 * i - SPREAD_FROM[i]
        want = jnp.where(within < 22, group * 22 + within + shift, -1)
        rows = lax.broadcasted_iota(jnp.int32, (512, ZB), 0)
        spread[i] = (rows == want).astype(F32).astype(BF16)

    def spread_cols(v):
        parts = []
        for i in range(4):
            lo = SPREAD_FROM[i]
            hi = min(lo + 512, D)
            parts.append(nn(v[:, lo:hi], spread[i, 0:hi - lo, :]).astype(BF16))
        return parts

    vis_row = visr[...]
    eye = lax.broadcasted_iota(jnp.int32, (ROWS, VIS), 0) == lax.broadcasted_iota(jnp.int32, (ROWS, VIS), 1)
    vis_col = jnp.sum(jnp.where(eye, vis_row + 1, 0), axis=1, keepdims=True) - 1
    vis_hit = lax.broadcasted_iota(jnp.int32, (ROWS, TUBES), 1) == vis_col
    vis_pick = vis_hit.astype(F32).astype(BF16)
    slot_of = jnp.sum(jnp.where(vis_hit, rank[...] + 1, 0), axis=1, keepdims=True) - 1
    own_pick = (lax.broadcasted_iota(jnp.int32, (ROWS, OWNP), 1) == slot_of).astype(F32).astype(BF16)

    swap.wait()
    gain_enc = genc[...].reshape(1, D).astype(F32)

    def all_tokens():
        mine = tokpad[...].astype(F32)
        theirs = tokrecv[...].astype(F32)
        xfull[:, 0:HALF] = jnp.where(first, mine, theirs)
        xfull[:, HALF:D] = jnp.where(first, theirs, mine)
        return xfull[...]

    normed, inv = norm_parts(all_tokens(), D)
    hidden = (normed * gain_enc).astype(BF16)
    for i, part in enumerate(spread_cols(hidden)):
        hid[:, i * ZB:(i + 1) * ZB] = part

    def send_hidden(g):
        axis = ROUTES[g][0]
        return [
            push(hid, hidg.at[g, d - 1], sh.at[g, d - 1], rh.at[g, d - 1], place_on[axis]((here[axis] + d) % 4))
            for d in range(1, 4)
        ]

    hid_sends = [None, None, send_hidden(2)]
    l_wt.wait()
    l_pos.start()
    l_dqkv.start()
    q = (nt(hidden, wt[0:HALF, :]) * ENC_SCALE).astype(BF16)
    k = nt(hidden, wt[HALF:2 * HALF, :]).astype(BF16)
    v = nt(hidden, wt[2 * HALF:3 * HALF, :]).astype(BF16)
    for h in range(HEADS):
        lanes = slice(h * HD, (h + 1) * HD)
        qs[h] = q[:, lanes]
        ks[h] = k[:, lanes]
        vs[h] = v[:, lanes]
    key_ok = lax.broadcasted_iota(jnp.int32, (ROWS, ROWS), 1) < VIS

    def enc_probs(h):
        s = jnp.where(key_ok, nt(qs[h], ks[h]), -1e30)
        e = jnp.exp(s - jnp.max(s, axis=-1, keepdims=True))
        return e * (1.0 / jnp.sum(e, axis=-1, keepdims=True))

    for h in range(HEADS):
        mixg[0, :, h * HD:(h + 1) * HD] = nn(enc_probs(h).astype(BF16), vs[h]).astype(BF16)
    l_proj.wait()
    heads_term = nn(mixg[0], proj[...])
    part_enc = (jnp.where(first, xfull[...], 0.0) + heads_term).astype(BF16)
    l_down.wait()
    lows[...] = nn(part_enc, down[...])
    swap = exchange(lows, lowr, 1)
    l_dproj.start()
    l_fc1.start()
    l_fc2.start()
    l_cot.start()

    swap.wait()
    mix_sends = [
        push(mixg.at[0], mixg.at[d], sm.at[d - 1], rm.at[d - 1], at_z((z + d) % 4)) for d in range(1, 4)
    ]
    hid_sends[0] = send_hidden(0)
    hid_sends[1] = send_hidden(1)
    lowered = (lows[...] + lowr[...]).astype(BF16)
    l_pos.wait()
    l_dqkv.wait()
    gain_one = gain1[...].reshape(1, DD).astype(F32)
    gain_two = gain2[...].reshape(1, DD).astype(F32)
    mask_row = maskt[...].reshape(1, DD).astype(F32)

    vd[...] = jnp.zeros((DH, TUBES, 128), BF16)
    vd[:, :, DHD:DHD + 1] = jnp.ones((DH, TUBES, 1), BF16)

    @pl.loop(0, 2)
    def _(b):
        rows = pl.ds(pl.multiple_of(b * OWN, 16), OWN)
        hit = lax.broadcasted_iota(jnp.int32, (OWN, VIS), 0) + b * OWN == vis_row
        hit = hit.astype(F32)
        placed = nn(hit.astype(BF16), lowered[0:VIS])
        covered = jnp.sum(hit, axis=1, keepdims=True)
        start = (placed + (1.0 - covered) * mask_row + pos[rows, :]).astype(BF16)
        xall[rows, :] = start
        n1, _ = norm_parts(start.astype(F32), DD)
        attn_in = (n1 * gain_one).astype(BF16)
        kv = nn(attn_in, dqkv[:, DI:3 * DI]).astype(BF16)
        kva[rows, :] = kv
        for h in range(DH):
            kd[h, rows, :] = kv[:, h * DHD:(h + 1) * DHD]
            vd[h, rows, 0:DHD] = kv[:, DI + h * DHD:DI + (h + 1) * DHD]

    for lo in (0, 400):
        rows = slice(lo, lo + 400)
        pick = lax.broadcasted_iota(jnp.int32, (400, TUBES), 0) + lo == rank[...]
        start = nn(pick.astype(F32).astype(BF16), xall[...])
        xown[rows, :] = start.astype(BF16)
        n1, _ = norm_parts(start, DD)
        attn_in = (n1 * gain_one).astype(BF16)
        q = (nn(attn_in, dqkv[:, 0:DI]) * DEC_SCALE).astype(BF16)
        qall[rows, :] = q
        for h in range(DH):
            qd[h, rows, :] = q[:, h * DHD:(h + 1) * DHD]

    @pl.loop(0, OWNP // QROWS)
    def _(b):
        rows = pl.ds(pl.multiple_of(b * QROWS, QROWS), QROWS)
        scores = [nt(qd[h, rows, :], kd[h]) for h in range(2)]
        for h in range(DH):
            s = scores[h]
            top = jnp.max(s, axis=-1, keepdims=True)
            if h + 2 < DH:
                scores.append(nt(qd[h + 2, rows, :], kd[h + 2]))
            e = jnp.exp(s - top).astype(BF16)
            o = nn(e, vd[h])
            total = 1.0 / o[:, DHD:DHD + 1]
            stat[rows, h:h + 1] = top
            stat[rows, 4 + h:5 + h] = total
            mixd[rows, h * DHD:(h + 1) * DHD] = o[:, 0:DHD] * total

    l_dproj.wait()

    for lo, hi in ((0, 400), (400, OWNP)):
        after = (xown[lo:hi, :].astype(F32) + nn(mixd[lo:hi, :].astype(BF16), dproj[...])).astype(BF16).astype(F32)
        n2, inv2 = norm_parts(after, DD)
        pos[lo:hi, :] = n2
        inv2s[lo:hi, :] = inv2
        mlp[lo:hi, :] = (n2 * gain_two).astype(BF16)

    l_fc1.wait()
    l_fc2.wait()
    l_cot.wait()
    held = None
    for c in range(DF // 512):
        part = slice(c * 512, (c + 1) * 512)
        up = nn(mlp[...], fc1[:, part])
        gact = nt(cot[...], fc2[part, :])
        if c == 1:
            pos[OWNP:, :] = nt(held, fc1[:, 0:512])
        elif c > 1:
            pos[OWNP:, :] += nt(held, fc1[:, (c - 1) * 512:c * 512])
        held = (gact * gelu_slope(up)).astype(BF16)
    pos[OWNP:, :] += nt(held, fc1[:, DF - 512:DF])

    for lo, hi in ((0, 400), (400, OWNP)):
        g = cot[lo:hi, :].astype(F32) + norm_back(pos[OWNP + lo:OWNP + hi, :], pos[lo:hi, :], inv2s[lo:hi, :], gain_two, DD)
        low = g.astype(BF16)
        gmid[lo:hi, :] = low
        gm = nt(low, dproj[...]).astype(BF16)
        gmall[lo:hi, :] = gm
        prod = gm.astype(F32) * mixd[lo:hi, :]
        for h in range(DH):
            lanes = slice(h * DHD, (h + 1) * DHD)
            gmix[h, lo:hi, :] = gm[:, lanes]
            stat[lo:hi, 8 + h:9 + h] = jnp.sum(prod[:, lanes], axis=-1, keepdims=True)

    vis_x = nn(vis_pick, xall[...])
    vis_kv = nn(vis_pick, kva[...]).astype(BF16)
    vis_q = nn(own_pick, qall[...]).astype(BF16)
    vis_g = nn(own_pick, gmall[...]).astype(BF16)
    exs[:, 3 * DI:] = nn(own_pick, gmid[...]).astype(BF16)
    for h in range(DH):
        lanes = slice(h * DHD, (h + 1) * DHD)
        k_vis = vis_kv[:, lanes]
        v_vis = vis_kv[:, DI + h * DHD:DI + (h + 1) * DHD]
        p = jnp.exp(nt(qd[h], k_vis) - stat[:, h:h + 1]) * stat[:, 4 + h:5 + h]
        ds = (p * (nt(gmix[h], v_vis) - stat[:, 8 + h:9 + h])).astype(BF16)
        exs[:, DI + h * DHD:DI + (h + 1) * DHD] = tn(ds, qd[h]).astype(BF16)
        exs[:, 2 * DI + h * DHD:2 * DI + (h + 1) * DHD] = tn(p.astype(BF16), gmix[h]).astype(BF16)
        s = nt(vis_q[:, lanes], kd[h])
        e = jnp.exp(s - jnp.max(s, axis=-1, keepdims=True))
        p = e * (1.0 / jnp.sum(e, axis=-1, keepdims=True))
        g = nt(vis_g[:, lanes], vd[h, :, 0:DHD])
        c = jnp.sum(p * g, axis=-1, keepdims=True)
        ds = (p * (g - c)).astype(BF16)
        exs[:, lanes] = (nn(ds, kd[h]) * DEC_SCALE).astype(BF16)

    swap = exchange(exs, exr, 2)
    swap.wait()
    both = exs[...].astype(F32) + exr[...].astype(F32)
    gattn = nt(both[:, 0:3 * DI].astype(BF16), dqkv[...])
    n1, inv1 = norm_parts(vis_x, DD)
    gstart = both[:, 3 * DI:] + norm_back(gattn, n1, inv1, gain_one, DD)
    real = lax.broadcasted_iota(jnp.int32, (ROWS, DD), 0) < VIS
    glow = jnp.where(real, gstart, 0.0).astype(BF16)

    genc_rows = nt(glow, down[...])
    gel = genc_rows.astype(BF16)
    for i, part in enumerate(spread_cols(gel)):
        gelp[i] = part
    gel_sends = []
    for d in range(1, 4):
        zi = (z + d) % 4
        gel_sends.append(push(gelp.at[zi], gelg.at[d], sg.at[d - 1], rg.at[d - 1], at_z(zi)))
    gelg[0] = gelp[z]
    gmx = nt(gel, proj[...]).astype(BF16)
    for h in range(HEADS):
        gms[h] = gmx[:, h * HD:(h + 1) * HD]
    for h in range(HEADS):
        p = enc_probs(h)
        gm = gms[h]
        g = nt(gm, vs[h])
        c = jnp.sum(p * g, axis=-1, keepdims=True)
        ds = (p * (g - c)).astype(BF16)
        three = ((nn(ds, ks[h]) * ENC_SCALE).astype(BF16), tn(ds, qs[h]).astype(BF16), tn(p.astype(BF16), gm).astype(BF16))
        lanes = slice((h % 2) * HD, (h % 2 + 1) * HD)
        for part in range(3):
            rq[part, h // 2, :, lanes] = three[part]
            gqkv[:, part * HALF + h * HD:part * HALF + (h + 1) * HD] = three[part]
    rq_sends = []
    for g in range(3):
        axis = ROUTES[g][0]
        sends = []
        for d in range(1, 4):
            i = (here[axis] + d) % 4
            sends.append(push(rq.at[g, i], rqg.at[g, d - 1], sq.at[g, d - 1], rqs.at[g, d - 1], place_on[axis](i)))
        rq_sends.append(sends)

    def total(mine, got):
        return (mine.astype(F32) + got[0].astype(F32)) + (got[1].astype(F32) + got[2].astype(F32))

    for copy in gel_sends:
        copy.wait()
    for copy in mix_sends:
        copy.wait()
    prod = tn(gelg[...].reshape(4 * ROWS, ZB), mixg[...].reshape(4 * ROWS, HALF)).astype(BF16).reshape(4, 4, 24, HALF)
    pa[...] = prod[:, :, :, 0:PA].reshape(4, 96, PA)
    for i in range(4):
        pb[i, :, :, 0:HALF - PA] = prod[:, i, :, PA:HALF]
        pb[i, :, :, HALF - PA:PA] = jnp.zeros((4, 24, 2 * PA - HALF), BF16)
    p_sends = []
    for d in range(1, 4):
        yi = (y + d) % 4
        xi = (x + d) % 4
        p_sends.append(push(pa.at[yi], qra.at[d - 1], s5.at[0, d - 1], r5.at[0, d - 1], at_y(yi)))
        p_sends.append(push(pb.at[xi], qrb.at[d - 1], s5.at[1, d - 1], r5.at[1, d - 1], at_x(xi)))

    terms = nn(gqkv[...], wt[...]).astype(BF16)
    scaled = terms.astype(F32) * gain_enc
    normed, inv = norm_parts(all_tokens(), D)
    s1 = jnp.sum(scaled, axis=-1, keepdims=True)
    s2 = jnp.sum(scaled * normed, axis=-1, keepdims=True)
    sts[...] = jnp.where(lax.broadcasted_iota(jnp.int32, (ROWS, 128), 1) == 0, s1, s2)
    hts[...] = jnp.where(first, terms[:, HALF:], terms[:, 0:HALF])
    swap_a = exchange(hts, htr, 3)
    swap_b = exchange(sts, strr, 4)

    second = []
    for g in range(3):
        gather, one, _ = ROUTES[g]
        for copy in hid_sends[g] + rq_sends[g]:
            copy.wait()
        prod = tn(hidg[g].reshape(3 * ROWS, PADW), rqg[g].reshape(3 * ROWS, HP)) + tn(hid[...], rq[g, here[gather]])
        cs[g] = prod.reshape(4, 4, 4, 24, HP).astype(BF16)
        for d in range(1, 4):
            i = (here[one] + d) % 4
            second.append(push(take(cs.at[g], one, i), ra.at[g, d - 1], sx.at[g, d - 1], rx.at[g, d - 1], place_on[one](i)))

    swap_a.wait()
    swap_b.wait()
    stats = sts[...] + strr[...]
    m1 = stats[:, 0:1] * (1.0 / D)
    m2 = stats[:, 1:2] * (1.0 / D)
    gh = jnp.where(first, terms[:, 0:HALF], terms[:, HALF:]).astype(F32) + htr[...].astype(F32)
    gain_mine = jnp.where(first, gain_enc[:, 0:HALF], gain_enc[:, HALF:])
    normed_mine = jnp.where(first, normed[:, 0:HALF], normed[:, HALF:])
    base = jnp.where(first, genc_rows[:, 0:HALF], genc_rows[:, HALF:D])
    out = base + inv * (gh * gain_mine - m1 - normed_mine * m2)
    gtok[...] = out[0:VIS, :]

    for copy in p_sends:
        copy.wait()
    qsa[...] = total(pa[y], qra).astype(BF16).reshape(4, 24, PA)
    qsb[...] = total(pb[x], qrb).astype(BF16)
    p_sends = []
    for d in range(1, 4):
        yi = (y + d) % 4
        xi = (x + d) % 4
        p_sends.append(push(qsa.at[xi], qta.at[d - 1], s6.at[0, d - 1], r6.at[0, d - 1], at_x(xi)))
        p_sends.append(push(qsb.at[yi], qtb.at[d - 1], s6.at[1, d - 1], r6.at[1, d - 1], at_y(yi)))

    third = []
    for g in range(3):
        gather, one, two = ROUTES[g]
        for copy in second[3 * g:3 * g + 3]:
            copy.wait()
        sa[g] = total(take(cs.at[g], one, here[one])[...], ra.at[g]).astype(BF16)
        rest = [axis for axis in range(3) if axis != one].index(two)
        for d in range(1, 4):
            i = (here[two] + d) % 4
            third.append(push(take(sa.at[g], rest, i), ta.at[g, d - 1], s3.at[g, d - 1], r3.at[g, d - 1], place_on[two](i)))
    for copy in p_sends:
        copy.wait()
    op[:, 0:PA] = total(qsa[x], qta)[0:22, :]
    op[:, PA:HALF] = total(qsb[y], qtb)[0:22, 0:HALF - PA]
    fourth = []
    for g in range(3):
        gather, one, two = ROUTES[g]
        for copy in third[3 * g:3 * g + 3]:
            copy.wait()
        rest = [axis for axis in range(3) if axis != one].index(two)
        fa[g] = total(take(sa.at[g], rest, here[two])[...], ta.at[g])
        for d in range(1, 4):
            i = (here[gather] + d) % 4
            fourth.append(push(fa.at[g, i], ga.at[g, here[gather]], s4.at[g, d - 1], r4.at[g, d - 1], place_on[gather](i)))
        ga[g, here[gather]] = fa[g, here[gather]]
    for copy in fourth:
        copy.wait()
    for g in range(3):
        for i in range(4):
            oq[g, :, HP * i:HP * (i + 1)] = ga[g, i][0:22, :]


def run_main(tok, visr, own, genc, maskt, gain1, gain2, wt, proj, down, dqkv, dproj, fc1, fc2, cot, pos):
    vm = pl.BlockSpec(memory_space=pltpu.VMEM)
    hbm = pl.BlockSpec(memory_space=pl.ANY)
    V = pltpu.VMEM
    S = pltpu.SemaphoreType.DMA
    big = (wt, proj, down, dqkv, dproj, fc1, fc2, cot, pos)
    half = (ROWS, HALF)
    scratch = [V(a.shape, a.dtype) for a in big[:7]] + [
        V((OWNP, DD), BF16), V((2 * OWNP, DD), F32),
        V(half, BF16), V(half, BF16), V((ROWS, D), F32),
        V((HEADS, ROWS, HD), BF16), V((HEADS, ROWS, HD), BF16), V((HEADS, ROWS, HD), BF16),
        V((HEADS, ROWS, HD), BF16),
        V((ROWS, DD), F32), V((ROWS, DD), F32), V((1, TUBES), jnp.int32), V((16, 128), F32), V((4, 512, ZB), BF16),
        V((TUBES, DD), BF16), V((DH, TUBES, DHD), BF16), V((DH, TUBES, 128), BF16), V((TUBES, 2 * DI), BF16),
        V((OWNP, DD), BF16), V((DH, OWNP, DHD), BF16), V((OWNP, DI), BF16), V((OWNP, DI), F32),
        V((OWNP, 16), F32),
        V((OWNP, DD), BF16), V((OWNP, 1), F32), V((OWNP, DD), BF16),
        V((DH, OWNP, DHD), BF16), V((OWNP, DI), BF16),
        V((ROWS, 3 * DI + DD), BF16), V((ROWS, 3 * DI + DD), BF16),
        V(half, BF16), V(half, BF16), V((ROWS, 128), F32), V((ROWS, 128), F32),
        V((ROWS, PADW), BF16), V((3, 3, ROWS, PADW), BF16),
        V((4, ROWS, HALF), BF16), V((4, ROWS, ZB), BF16), V((4, ROWS, ZB), BF16),
        V((3, 4, ROWS, HP), BF16), V((ROWS, 3 * HALF), BF16), V((3, 3, ROWS, HP), BF16),
        V((3, 4, 4, 4, 24, HP), BF16), V((3, 3, 4, 4, 24, HP), BF16),
        V((3, 4, 4, 24, HP), BF16), V((3, 3, 4, 24, HP), BF16), V((3, 4, 24, HP), F32), V((3, 4, 24, HP), F32),
        V((4, 96, PA), BF16), V((4, 4, 24, PA), BF16), V((3, 96, PA), BF16), V((3, 4, 24, PA), BF16),
        V((4, 24, PA), BF16), V((4, 24, PA), BF16), V((3, 24, PA), BF16), V((3, 24, PA), BF16),
        S((9,)), S((5,)), S((5,)), S((3, 3)), S((3, 3)), S((3,)), S((3,)), S((3,)), S((3,)), S((3, 3)), S((3, 3)),
        S((3, 3)), S((3, 3)), S((3, 3)), S((3, 3)), S((3, 3)), S((3, 3)),
        S((2, 3)), S((2, 3)), S((2, 3)), S((2, 3)),
    ]
    return pl.pallas_call(
        main_kernel,
        out_shape=(
            jax.ShapeDtypeStruct((VIS, HALF), F32),
            jax.ShapeDtypeStruct((3, 22, HALF), F32),
            jax.ShapeDtypeStruct((22, HALF), F32),
        ),
        in_specs=[vm] * 7 + [hbm] * 9,
        out_specs=[vm] * 3,
        scratch_shapes=scratch,
        compiler_params=pltpu.CompilerParams(
            collective_id=0, has_side_effects=True, vmem_limit_bytes=60 * 1024 * 1024
        ),
    )(tok, visr, own, genc, maskt, gain1, gain2, *big)


def finish_kernel(gtok, gq, gp, tok_o, q_o, p_o):
    tok_o[...] = gtok[...].reshape(VIS, 1, HALF)
    q_o[...] = gq[...]
    p_o[...] = gp[...]


def finish(gtok, gq, gp):
    vm = pl.BlockSpec(memory_space=pltpu.VMEM)
    return pl.pallas_call(
        finish_kernel,
        out_shape=(
            jax.ShapeDtypeStruct((VIS, 1, HALF), F32),
            jax.ShapeDtypeStruct((3, 22, HALF), F32),
            jax.ShapeDtypeStruct((22, HALF), F32),
        ),
        in_specs=[vm] * 3,
        out_specs=[vm] * 3,
    )(gtok, gq, gp)


def per_device(
    tokens, vis_index, owner, enc_gain, enc_qkv, enc_proj, to_decoder, mask_token, dec_gain1,
    dec_qkv, dec_proj, dec_gain2, dec_fc1, dec_fc2, cotangent,
):
    wt = jnp.transpose(enc_qkv, (1, 2, 0)).reshape(3 * HALF, D)
    gtok, gq, gp = run_main(
        tokens[0], vis_index, owner, enc_gain, mask_token, dec_gain1, dec_gain2, wt, enc_proj,
        to_decoder, dec_qkv, dec_proj, dec_fc1, dec_fc2, cotangent[0], jnp.asarray(position_rows()),
    )
    gtok, gq, gp = finish(gtok, gq, gp)
    return jnp.transpose(gtok, (1, 0, 2)), jnp.transpose(gq, (1, 0, 2)), jnp.transpose(gp)


def solution(mesh):
    return jax.shard_map(
        per_device,
        mesh=mesh,
        in_specs=(
            P("dp", None, "fsdp"),
            P("dp", None),
            P("dp", None),
            P(),
            P(None, None, "fsdp"),
            P("fsdp", None),
            P(),
            P(),
            P(),
            P(),
            P(),
            P(),
            P(),
            P(),
            P("dp", "fsdp", None),
        ),
        out_specs=(P("dp", None, "fsdp"), P("dp", None, "fsdp"), P("fsdp", "dp")),
        check_vma=False,
    )
```

```python
import functools
import math

import jax
import jax.numpy as jnp
import numpy as np
from jax import lax
from jax.experimental import pallas as pl
from jax.experimental.pallas import tpu as pltpu
from jax.sharding import PartitionSpec as P

D = 1408
HALF = 704
HD = 88
HEADS = 8
DD = 512
DHD = 64
DH = 4
DI = 256
DF = 2048
TUBES = 1568
VIS = 157
ROWS = 160
OWN = 784
OWNP = 800
QROWS = 160
PADW = 1536
ZB = 384
PA = 384
HP = 176
EPS = 1e-06
ENC_SCALE = HD ** (-0.5)
DEC_SCALE = DHD ** (-0.5)
SQRT_HALF = 0.7071067811865476
INV_SQRT_TWO_PI = 0.3989422804014327
F32 = jnp.float32
BF16 = jnp.bfloat16
MESH = pl.DeviceIdType.MESH
SPREAD_FROM = (0, 256, 640, 1024)
ROUTES = ((2, 1, 0), (1, 0, 2), (0, 2, 1))


def nn(a, b):
    return lax.dot_general(a, b, (((1,), (0,)), ((), ())), preferred_element_type=F32)


def nt(a, b):
    return lax.dot_general(a, b, (((1,), (1,)), ((), ())), preferred_element_type=F32)


def tn(a, b):
    return lax.dot_general(a, b, (((0,), (0,)), ((), ())), preferred_element_type=F32)


def norm_parts(values, width):
    mean = jnp.sum(values, axis=-1, keepdims=True) * (1.0 / width)
    centred = values - mean
    inv = lax.rsqrt(jnp.sum(centred * centred, axis=-1, keepdims=True) * (1.0 / width) + EPS)
    return centred * inv, inv


def norm_back(grad, normed, inv, gain, width):
    scaled = grad * gain
    first = jnp.sum(scaled, axis=-1, keepdims=True) * (1.0 / width)
    second = jnp.sum(scaled * normed, axis=-1, keepdims=True) * (1.0 / width)
    return inv * (scaled - first - normed * second)


def gelu_slope(u):
    return 0.5 * (1.0 + lax.erf(u * SQRT_HALF)) + u * jnp.exp(-0.5 * u * u) * INV_SQRT_TWO_PI


def position_rows():
    rates = np.exp(np.arange(DD // 2, dtype=np.float32) * np.float32(-2.0 * math.log(10000.0) / DD))
    angles = np.arange(TUBES, dtype=np.float32)[:, None] * rates
    return np.stack([np.sin(angles), np.cos(angles)], axis=-1).reshape(TUBES, DD).astype(np.float32)


def main_kernel(
    tok, visr, own, genc, maskt, gain1, gain2,
    wt_h, proj_h, down_h, dqkv_h, dproj_h, fc1_h, fc2_h, cot_h, pos_h,
    gtok, oq, op,
    wt, proj, down, dqkv, dproj, fc1, fc2, cot, pos,
    tokpad, tokrecv, xfull, qs, ks, vs, gms, lows, lowr, rank, rtile, spread,
    xall, kd, vd, kva, xown, qd, qall, mixd, stat, mlp, inv2s, gmix, gmall,
    exs, exr, hts, htr, sts, strr,
    hid, hidg, mixg, gelp, gelg, rq, gqkv, rqg,
    cs0, cs1, cs2, ra0, ra1, ra2, sa0, sa1, sa2, ta, fa, ga, probs, invs,
    pa, pb, qra, qrb, qsa, qsb, qta, qtb,
    local, send, recv, sh, rh, sm, rm, sg, rg, sq, rqs,
    sx, rx, s3, r3, s4, r4, s5, r5, s6, r6,
):
    me = lax.axis_index("fsdp")
    dp = lax.axis_index("dp")
    z = dp // 16
    y = (dp // 4) % 4
    x = dp % 4
    other = 1 - me
    first = me == 0

    def at_x(i):
        return (z * 16 + y * 4 + i, me)

    def at_y(i):
        return (z * 16 + i * 4 + x, me)

    def at_z(i):
        return (i * 16 + y * 4 + x, me)

    place_on = (at_z, at_y, at_x)
    here = (z, y, x)

    cs, ra, sa = (cs0, cs1, cs2), (ra0, ra1, ra2), (sa0, sa1, sa2)

    def take(ref, axis, i):
        if axis == 0:
            return ref.at[i]
        return ref.at[:, i] if axis == 1 else ref.at[:, :, i]

    loads = [
        pltpu.make_async_copy(src, dst, local.at[i])
        for i, (src, dst) in enumerate(
            [(wt_h, wt), (proj_h, proj), (down_h, down), (pos_h, pos.at[0:TUBES]), (dqkv_h, dqkv),
             (dproj_h, dproj), (fc1_h, fc1), (fc2_h, fc2), (cot_h, cot.at[0:OWN])]
        )
    ]
    l_wt, l_proj, l_down, l_pos, l_dqkv, l_dproj, l_fc1, l_fc2, l_cot = loads
    l_wt.start()
    l_proj.start()
    l_down.start()

    def push(src, dst, ssem, rsem, place):
        copy = pltpu.make_async_remote_copy(
            src_ref=src, dst_ref=dst, send_sem=ssem, recv_sem=rsem, device_id=place, device_id_type=MESH
        )
        copy.start()
        return copy

    def exchange(src, dst, i):
        return push(src, dst, send.at[i], recv.at[i], (dp, other))

    barrier = pltpu.get_barrier_semaphore()
    pl.semaphore_signal(barrier, inc=1, device_id=(dp, other), device_id_type=MESH)
    for d in range(1, 4):
        for place in (at_x((x + d) % 4), at_y((y + d) % 4), at_z((z + d) % 4)):
            pl.semaphore_signal(barrier, inc=1, device_id=place, device_id_type=MESH)

    cot[OWN:OWNP, :] = jnp.zeros((OWNP - OWN, DD), BF16)
    tokpad[...] = jnp.zeros((ROWS, HALF), BF16)
    tokpad[0:VIS, :] = tok[...]
    pl.semaphore_wait(barrier, 10)
    swap = exchange(tokpad, tokrecv, 0)

    mine_row = (own[...] == me).astype(F32)
    rtile[...] = jnp.zeros((16, 128), F32)
    for i in range(13):
        wide = min(128, TUBES - 128 * i)
        rtile[i:i + 1, 0:wide] = mine_row[:, 128 * i:128 * i + wide]
    tiles = rtile[...]
    upper = lax.broadcasted_iota(jnp.int32, (128, 128), 0) <= lax.broadcasted_iota(jnp.int32, (128, 128), 1)
    inside = nn(tiles.astype(BF16), upper.astype(F32).astype(BF16))
    lower = lax.broadcasted_iota(jnp.int32, (16, 16), 0) > lax.broadcasted_iota(jnp.int32, (16, 16), 1)
    before = nn(lower.astype(F32).astype(BF16), jnp.broadcast_to(inside[:, 127:128], (16, 128)).astype(BF16))
    rtile[...] = jnp.where(tiles > 0.0, inside + before, 0.0)
    for i in range(13):
        wide = min(128, TUBES - 128 * i)
        rank[:, 128 * i:128 * i + wide] = rtile[i:i + 1, 0:wide].astype(jnp.int32) - 1

    lane = lax.broadcasted_iota(jnp.int32, (1, ZB), 1)
    group = (lane.astype(F32) * (1.0 / 24.0) + 0.01).astype(jnp.int32)
    within = lane - group * 24
    for i in range(4):
        shift = 352 * i - SPREAD_FROM[i]
        want = jnp.where(within < 22, group * 22 + within + shift, -1)
        rows = lax.broadcasted_iota(jnp.int32, (512, ZB), 0)
        spread[i] = (rows == want).astype(F32).astype(BF16)

    def spread_cols(v):
        parts = []
        for i in range(4):
            lo = SPREAD_FROM[i]
            hi = min(lo + 512, D)
            parts.append(nn(v[:, lo:hi], spread[i, 0:hi - lo, :]).astype(BF16))
        return parts

    vis_row = visr[...]
    eye = lax.broadcasted_iota(jnp.int32, (ROWS, VIS), 0) == lax.broadcasted_iota(jnp.int32, (ROWS, VIS), 1)
    vis_col = jnp.sum(jnp.where(eye, vis_row + 1, 0), axis=1, keepdims=True) - 1
    vis_hit = lax.broadcasted_iota(jnp.int32, (ROWS, TUBES), 1) == vis_col
    vis_pick = vis_hit.astype(F32).astype(BF16)
    slot_of = jnp.sum(jnp.where(vis_hit, rank[...] + 1, 0), axis=1, keepdims=True) - 1
    own_pick = (lax.broadcasted_iota(jnp.int32, (ROWS, OWNP), 1) == slot_of).astype(F32).astype(BF16)

    swap.wait()
    gain_enc = genc[...].reshape(1, D).astype(F32)

    def all_tokens():
        mine = tokpad[...].astype(F32)
        theirs = tokrecv[...].astype(F32)
        xfull[:, 0:HALF] = jnp.where(first, mine, theirs)
        xfull[:, HALF:D] = jnp.where(first, theirs, mine)
        return xfull[...]

    normed, inv = norm_parts(all_tokens(), D)
    invs[...] = inv
    hidden = (normed * gain_enc).astype(BF16)
    for i, part in enumerate(spread_cols(hidden)):
        hid[:, i * ZB:(i + 1) * ZB] = part

    def send_hidden(g):
        axis = ROUTES[g][0]
        return [
            push(hid, hidg.at[g, d - 1], sh.at[g, d - 1], rh.at[g, d - 1], place_on[axis]((here[axis] + d) % 4))
            for d in range(1, 4)
        ]

    hid_sends = [None, None, send_hidden(2)]
    l_wt.wait()
    l_pos.start()
    l_dqkv.start()
    q = (nt(hidden, wt[0:HALF, :]) * ENC_SCALE).astype(BF16)
    k = nt(hidden, wt[HALF:2 * HALF, :]).astype(BF16)
    v = nt(hidden, wt[2 * HALF:3 * HALF, :]).astype(BF16)
    for h in range(HEADS):
        lanes = slice(h * HD, (h + 1) * HD)
        qs[h] = q[:, lanes]
        ks[h] = k[:, lanes]
        vs[h] = v[:, lanes]
    key_ok = lax.broadcasted_iota(jnp.int32, (ROWS, ROWS), 1) < VIS

    def enc_probs(h):
        s = jnp.where(key_ok, nt(qs[h], ks[h]), -1e30)
        e = jnp.exp(s - jnp.max(s, axis=-1, keepdims=True))
        return e * (1.0 / jnp.sum(e, axis=-1, keepdims=True))

    for h in range(HEADS):
        p = enc_probs(h)
        probs[h] = p
        mixg[0, :, h * HD:(h + 1) * HD] = nn(p.astype(BF16), vs[h]).astype(BF16)
    l_proj.wait()
    heads_term = nn(mixg[0], proj[...])
    part_enc = (jnp.where(first, xfull[...], 0.0) + heads_term).astype(BF16)
    l_down.wait()
    lows[...] = nn(part_enc, down[...])
    swap = exchange(lows, lowr, 1)
    l_dproj.start()
    l_fc1.start()
    l_fc2.start()
    l_cot.start()

    swap.wait()
    mix_sends = [
        push(mixg.at[0], mixg.at[d], sm.at[d - 1], rm.at[d - 1], at_z((z + d) % 4)) for d in range(1, 4)
    ]
    hid_sends[0] = send_hidden(0)
    hid_sends[1] = send_hidden(1)
    lowered = (lows[...] + lowr[...]).astype(BF16)
    l_pos.wait()
    l_dqkv.wait()
    gain_one = gain1[...].reshape(1, DD).astype(F32)
    gain_two = gain2[...].reshape(1, DD).astype(F32)
    mask_row = maskt[...].reshape(1, DD).astype(F32)

    vd[...] = jnp.zeros((DH, TUBES, 128), BF16)
    vd[:, :, DHD:DHD + 1] = jnp.ones((DH, TUBES, 1), BF16)

    @pl.loop(0, 2)
    def _(b):
        rows = pl.ds(pl.multiple_of(b * OWN, 16), OWN)
        hit = lax.broadcasted_iota(jnp.int32, (OWN, VIS), 0) + b * OWN == vis_row
        hit = hit.astype(F32)
        placed = nn(hit.astype(BF16), lowered[0:VIS])
        covered = jnp.sum(hit, axis=1, keepdims=True)
        start = (placed + (1.0 - covered) * mask_row + pos[rows, :]).astype(BF16)
        xall[rows, :] = start
        n1, _ = norm_parts(start.astype(F32), DD)
        attn_in = (n1 * gain_one).astype(BF16)
        kv = nn(attn_in, dqkv[:, DI:3 * DI]).astype(BF16)
        kva[rows, :] = kv
        for h in range(DH):
            kd[h, rows, :] = kv[:, h * DHD:(h + 1) * DHD]
            vd[h, rows, 0:DHD] = kv[:, DI + h * DHD:DI + (h + 1) * DHD]

    for lo in (0, 400):
        rows = slice(lo, lo + 400)
        pick = lax.broadcasted_iota(jnp.int32, (400, TUBES), 0) + lo == rank[...]
        start = nn(pick.astype(F32).astype(BF16), xall[...])
        xown[rows, :] = start.astype(BF16)
        n1, _ = norm_parts(start, DD)
        attn_in = (n1 * gain_one).astype(BF16)
        q = (nn(attn_in, dqkv[:, 0:DI]) * DEC_SCALE).astype(BF16)
        qall[rows, :] = q
        for h in range(DH):
            qd[h, rows, :] = q[:, h * DHD:(h + 1) * DHD]

    @pl.loop(0, OWNP // QROWS)
    def _(b):
        rows = pl.ds(pl.multiple_of(b * QROWS, QROWS), QROWS)
        scores = [nt(qd[h, rows, :], kd[h]) for h in range(2)]
        for h in range(DH):
            s = scores[h]
            top = jnp.max(s, axis=-1, keepdims=True)
            if h + 2 < DH:
                scores.append(nt(qd[h + 2, rows, :], kd[h + 2]))
            e = jnp.exp(s - top).astype(BF16)
            o = nn(e, vd[h])
            total = 1.0 / o[:, DHD:DHD + 1]
            stat[rows, h:h + 1] = top
            stat[rows, 4 + h:5 + h] = total
            mixd[rows, h * DHD:(h + 1) * DHD] = o[:, 0:DHD] * total

    l_dproj.wait()

    for lo, hi in ((0, 400), (400, OWNP)):
        after = (xown[lo:hi, :].astype(F32) + nn(mixd[lo:hi, :].astype(BF16), dproj[...])).astype(BF16).astype(F32)
        n2, inv2 = norm_parts(after, DD)
        pos[lo:hi, :] = n2
        inv2s[lo:hi, :] = inv2
        mlp[lo:hi, :] = (n2 * gain_two).astype(BF16)

    l_fc1.wait()
    l_fc2.wait()
    l_cot.wait()
    held = None
    for c in range(DF // 512):
        part = slice(c * 512, (c + 1) * 512)
        up = nn(mlp[...], fc1[:, part])
        gact = nt(cot[...], fc2[part, :])
        if c == 1:
            pos[OWNP:, :] = nt(held, fc1[:, 0:512])
        elif c > 1:
            pos[OWNP:, :] += nt(held, fc1[:, (c - 1) * 512:c * 512])
        held = (gact * gelu_slope(up)).astype(BF16)
    pos[OWNP:, :] += nt(held, fc1[:, DF - 512:DF])

    for lo, hi in ((0, 400), (400, OWNP)):
        g = cot[lo:hi, :].astype(F32) + norm_back(pos[OWNP + lo:OWNP + hi, :], pos[lo:hi, :], inv2s[lo:hi, :], gain_two, DD)
        low = g.astype(BF16)
        mlp[lo:hi, :] = low
        gm = nt(low, dproj[...]).astype(BF16)
        gmall[lo:hi, :] = gm
        prod = gm.astype(F32) * mixd[lo:hi, :]
        for h in range(DH):
            lanes = slice(h * DHD, (h + 1) * DHD)
            gmix[h, lo:hi, :] = gm[:, lanes]
            stat[lo:hi, 8 + h:9 + h] = jnp.sum(prod[:, lanes], axis=-1, keepdims=True)

    vis_x = nn(vis_pick, xall[...])
    vis_kv = nn(vis_pick, kva[...]).astype(BF16)
    vis_q = nn(own_pick, qall[...]).astype(BF16)
    vis_g = nn(own_pick, gmall[...]).astype(BF16)
    exs[:, 3 * DI:] = nn(own_pick, mlp[...]).astype(BF16)
    for h in range(DH):
        lanes = slice(h * DHD, (h + 1) * DHD)
        k_vis = vis_kv[:, lanes]
        v_vis = vis_kv[:, DI + h * DHD:DI + (h + 1) * DHD]
        p = jnp.exp(nt(qd[h], k_vis) - stat[:, h:h + 1]) * stat[:, 4 + h:5 + h]
        ds = (p * (nt(gmix[h], v_vis) - stat[:, 8 + h:9 + h])).astype(BF16)
        exs[:, DI + h * DHD:DI + (h + 1) * DHD] = tn(ds, qd[h]).astype(BF16)
        exs[:, 2 * DI + h * DHD:2 * DI + (h + 1) * DHD] = tn(p.astype(BF16), gmix[h]).astype(BF16)
        s = nt(vis_q[:, lanes], kd[h])
        e = jnp.exp(s - jnp.max(s, axis=-1, keepdims=True))
        p = e * (1.0 / jnp.sum(e, axis=-1, keepdims=True))
        g = nt(vis_g[:, lanes], vd[h, :, 0:DHD])
        c = jnp.sum(p * g, axis=-1, keepdims=True)
        ds = (p * (g - c)).astype(BF16)
        exs[:, lanes] = (nn(ds, kd[h]) * DEC_SCALE).astype(BF16)

    swap = exchange(exs, exr, 2)
    swap.wait()
    both = exs[...].astype(F32) + exr[...].astype(F32)
    gattn = nt(both[:, 0:3 * DI].astype(BF16), dqkv[...])
    n1, inv1 = norm_parts(vis_x, DD)
    gstart = both[:, 3 * DI:] + norm_back(gattn, n1, inv1, gain_one, DD)
    real = lax.broadcasted_iota(jnp.int32, (ROWS, DD), 0) < VIS
    glow = jnp.where(real, gstart, 0.0).astype(BF16)

    genc_rows = nt(glow, down[...])
    gel = genc_rows.astype(BF16)
    for i, part in enumerate(spread_cols(gel)):
        gelp[i] = part
    gel_sends = []
    for d in range(1, 4):
        zi = (z + d) % 4
        gel_sends.append(push(gelp.at[zi], gelg.at[d], sg.at[d - 1], rg.at[d - 1], at_z(zi)))
    gelg[0] = gelp[z]
    gmx = nt(gel, proj[...]).astype(BF16)
    for h in range(HEADS):
        gms[h] = gmx[:, h * HD:(h + 1) * HD]
    def send_rows(g):
        axis = ROUTES[g][0]
        sends = []
        for d in range(1, 4):
            i = (here[axis] + d) % 4
            sends.append(push(rq.at[g, i], rqg.at[g, d - 1], sq.at[g, d - 1], rqs.at[g, d - 1], place_on[axis](i)))
        return sends

    def keep_rows(part, h, rows):
        rq[part, h // 2, :, (h % 2) * HD:(h % 2 + 1) * HD] = rows
        gqkv[:, part * HALF + h * HD:part * HALF + (h + 1) * HD] = rows

    for h in range(HEADS):
        keep_rows(2, h, tn(probs[h].astype(BF16), gms[h]).astype(BF16))
    rq_sends = [None, None, send_rows(2)]
    for h in range(HEADS):
        p = probs[h]
        g = nt(gms[h], vs[h])
        c = jnp.sum(p * g, axis=-1, keepdims=True)
        ds = (p * (g - c)).astype(BF16)
        keep_rows(0, h, (nn(ds, ks[h]) * ENC_SCALE).astype(BF16))
        keep_rows(1, h, tn(ds, qs[h]).astype(BF16))
    rq_sends[0] = send_rows(0)
    rq_sends[1] = send_rows(1)

    def total(mine, got):
        return (mine.astype(F32) + got[0].astype(F32)) + (got[1].astype(F32) + got[2].astype(F32))

    for copy in gel_sends:
        copy.wait()
    for copy in mix_sends:
        copy.wait()
    prod = tn(gelg[...].reshape(4 * ROWS, ZB), mixg[...].reshape(4 * ROWS, HALF)).astype(BF16).reshape(4, 4, 24, HALF)
    pa[...] = prod[:, :, :, 0:PA].reshape(4, 96, PA)
    for i in range(4):
        pb[i, :, :, 0:HALF - PA] = prod[:, i, :, PA:HALF]
        pb[i, :, :, HALF - PA:PA] = jnp.zeros((4, 24, 2 * PA - HALF), BF16)
    p_sends = []
    for d in range(1, 4):
        yi = (y + d) % 4
        xi = (x + d) % 4
        p_sends.append(push(pa.at[yi], qra.at[d - 1], s5.at[0, d - 1], r5.at[0, d - 1], at_y(yi)))
        p_sends.append(push(pb.at[xi], qrb.at[d - 1], s5.at[1, d - 1], r5.at[1, d - 1], at_x(xi)))

    def first_sum(g):
        gather, one, _ = ROUTES[g]
        for copy in hid_sends[g] + rq_sends[g]:
            copy.wait()
        prod = tn(hidg[g].reshape(3 * ROWS, PADW), rqg[g].reshape(3 * ROWS, HP)) + tn(hid[...], rq[g, here[gather]])
        prod = prod.astype(BF16).reshape(4, 4, 4, 24, HP)
        for i in range(4):
            lanes = slice((i % 2) * HP, (i % 2 + 1) * HP)
            if gather == 0:
                cs[g][i // 2, :, :, :, lanes] = prod[i]
            elif gather == 1:
                cs[g][:, i // 2, :, :, lanes] = prod[:, i]
            else:
                cs[g][:, :, i // 2, :, lanes] = prod[:, :, i]
        sends = []
        for d in range(1, 4):
            i = (here[one] + d) % 4
            sends.append(push(take(cs[g], one, i), ra[g].at[d - 1], sx.at[g, d - 1], rx.at[g, d - 1], place_on[one](i)))
        return sends

    second = [None, None, first_sum(2)]

    terms = nn(gqkv[...], wt[...]).astype(BF16)
    scaled = terms.astype(F32) * gain_enc
    normed, _ = norm_parts(all_tokens(), D)
    inv = invs[...]
    s1 = jnp.sum(scaled, axis=-1, keepdims=True)
    s2 = jnp.sum(scaled * normed, axis=-1, keepdims=True)
    sts[...] = jnp.where(lax.broadcasted_iota(jnp.int32, (ROWS, 128), 1) == 0, s1, s2)
    hts[...] = jnp.where(first, terms[:, HALF:], terms[:, 0:HALF])
    swap_a = exchange(hts, htr, 3)
    swap_b = exchange(sts, strr, 4)

    second[0] = first_sum(0)
    second[1] = first_sum(1)

    swap_a.wait()
    swap_b.wait()
    stats = sts[...] + strr[...]
    m1 = stats[:, 0:1] * (1.0 / D)
    m2 = stats[:, 1:2] * (1.0 / D)
    gh = jnp.where(first, terms[:, 0:HALF], terms[:, HALF:]).astype(F32) + htr[...].astype(F32)
    gain_mine = jnp.where(first, gain_enc[:, 0:HALF], gain_enc[:, HALF:])
    normed_mine = jnp.where(first, normed[:, 0:HALF], normed[:, HALF:])
    base = jnp.where(first, genc_rows[:, 0:HALF], genc_rows[:, HALF:D])
    out = base + inv * (gh * gain_mine - m1 - normed_mine * m2)
    gtok[...] = out[0:VIS, :]

    for copy in p_sends:
        copy.wait()
    qsa[...] = total(pa[y], qra).astype(BF16).reshape(4, 24, PA)
    qsb[...] = total(pb[x], qrb).astype(BF16)
    p_sends = []
    for d in range(1, 4):
        yi = (y + d) % 4
        xi = (x + d) % 4
        p_sends.append(push(qsa.at[xi], qta.at[d - 1], s6.at[0, d - 1], r6.at[0, d - 1], at_x(xi)))
        p_sends.append(push(qsb.at[yi], qtb.at[d - 1], s6.at[1, d - 1], r6.at[1, d - 1], at_y(yi)))

    third = [None, None, None]
    for g in (2, 0, 1):
        gather, one, two = ROUTES[g]
        for copy in second[g]:
            copy.wait()
        sa[g][...] = total(take(cs[g], one, here[one])[...], ra[g]).astype(BF16)
        rest = [axis for axis in range(3) if axis != one].index(two)
        third[g] = []
        for d in range(1, 4):
            i = (here[two] + d) % 4
            third[g].append(push(take(sa[g], rest, i), ta.at[g, d - 1], s3.at[g, d - 1], r3.at[g, d - 1], place_on[two](i)))
    for copy in p_sends:
        copy.wait()
    op[:, 0:PA] = total(qsa[x], qta)[0:22, :]
    op[:, PA:HALF] = total(qsb[y], qtb)[0:22, 0:HALF - PA]
    fourth = []
    for g in (2, 0, 1):
        gather, one, two = ROUTES[g]
        for copy in third[g]:
            copy.wait()
        rest = [axis for axis in range(3) if axis != one].index(two)
        sums = total(take(sa[g], rest, here[two])[...], ta.at[g])
        for i in range(4):
            fa[g, i] = sums[i // 2, :, (i % 2) * HP:(i % 2 + 1) * HP]
        for d in range(1, 4):
            i = (here[gather] + d) % 4
            fourth.append(push(fa.at[g, i], ga.at[g, here[gather]], s4.at[g, d - 1], r4.at[g, d - 1], place_on[gather](i)))
        ga[g, here[gather]] = fa[g, here[gather]]
    for copy in fourth:
        copy.wait()
    for g in range(3):
        for i in range(4):
            oq[g, :, HP * i:HP * (i + 1)] = ga[g, i][0:22, :]


def run_main(tok, visr, own, genc, maskt, gain1, gain2, wt, proj, down, dqkv, dproj, fc1, fc2, cot, pos):
    vm = pl.BlockSpec(memory_space=pltpu.VMEM)
    hbm = pl.BlockSpec(memory_space=pl.ANY)
    V = pltpu.VMEM
    S = pltpu.SemaphoreType.DMA
    big = (wt, proj, down, dqkv, dproj, fc1, fc2, cot, pos)
    half = (ROWS, HALF)
    scratch = [V(a.shape, a.dtype) for a in big[:7]] + [
        V((OWNP, DD), BF16), V((2 * OWNP, DD), F32),
        V(half, BF16), V(half, BF16), V((ROWS, D), F32),
        V((HEADS, ROWS, HD), BF16), V((HEADS, ROWS, HD), BF16), V((HEADS, ROWS, HD), BF16),
        V((HEADS, ROWS, HD), BF16),
        V((ROWS, DD), F32), V((ROWS, DD), F32), V((1, TUBES), jnp.int32), V((16, 128), F32), V((4, 512, ZB), BF16),
        V((TUBES, DD), BF16), V((DH, TUBES, DHD), BF16), V((DH, TUBES, 128), BF16), V((TUBES, 2 * DI), BF16),
        V((OWNP, DD), BF16), V((DH, OWNP, DHD), BF16), V((OWNP, DI), BF16), V((OWNP, DI), F32),
        V((OWNP, 16), F32),
        V((OWNP, DD), BF16), V((OWNP, 1), F32),
        V((DH, OWNP, DHD), BF16), V((OWNP, DI), BF16),
        V((ROWS, 3 * DI + DD), BF16), V((ROWS, 3 * DI + DD), BF16),
        V(half, BF16), V(half, BF16), V((ROWS, 128), F32), V((ROWS, 128), F32),
        V((ROWS, PADW), BF16), V((3, 3, ROWS, PADW), BF16),
        V((4, ROWS, HALF), BF16), V((4, ROWS, ZB), BF16), V((4, ROWS, ZB), BF16),
        V((3, 4, ROWS, HP), BF16), V((ROWS, 3 * HALF), BF16), V((3, 3, ROWS, HP), BF16),
        V((4, 4, 2, 24, 2 * HP), BF16), V((4, 2, 4, 24, 2 * HP), BF16), V((2, 4, 4, 24, 2 * HP), BF16),
        V((3, 4, 2, 24, 2 * HP), BF16), V((3, 2, 4, 24, 2 * HP), BF16), V((3, 2, 4, 24, 2 * HP), BF16),
        V((4, 2, 24, 2 * HP), BF16), V((2, 4, 24, 2 * HP), BF16), V((2, 4, 24, 2 * HP), BF16),
        V((3, 3, 2, 24, 2 * HP), BF16), V((3, 4, 24, HP), F32), V((3, 4, 24, HP), F32),
        V((HEADS, ROWS, ROWS), F32), V((ROWS, 1), F32),
        V((4, 96, PA), BF16), V((4, 4, 24, PA), BF16), V((3, 96, PA), BF16), V((3, 4, 24, PA), BF16),
        V((4, 24, PA), BF16), V((4, 24, PA), BF16), V((3, 24, PA), BF16), V((3, 24, PA), BF16),
        S((9,)), S((5,)), S((5,)), S((3, 3)), S((3, 3)), S((3,)), S((3,)), S((3,)), S((3,)), S((3, 3)), S((3, 3)),
        S((3, 3)), S((3, 3)), S((3, 3)), S((3, 3)), S((3, 3)), S((3, 3)),
        S((2, 3)), S((2, 3)), S((2, 3)), S((2, 3)),
    ]
    return pl.pallas_call(
        main_kernel,
        out_shape=(
            jax.ShapeDtypeStruct((VIS, HALF), F32),
            jax.ShapeDtypeStruct((3, 22, HALF), F32),
            jax.ShapeDtypeStruct((22, HALF), F32),
        ),
        in_specs=[vm] * 7 + [hbm] * 9,
        out_specs=[vm] * 3,
        scratch_shapes=scratch,
        compiler_params=pltpu.CompilerParams(
            collective_id=0, has_side_effects=True, vmem_limit_bytes=60 * 1024 * 1024
        ),
    )(tok, visr, own, genc, maskt, gain1, gain2, *big)


def finish_kernel(gtok, gq, gp, tok_o, q_o, p_o):
    tok_o[...] = gtok[...].reshape(VIS, 1, HALF)
    q_o[...] = gq[...]
    p_o[...] = gp[...]


def finish(gtok, gq, gp):
    vm = pl.BlockSpec(memory_space=pltpu.VMEM)
    return pl.pallas_call(
        finish_kernel,
        out_shape=(
            jax.ShapeDtypeStruct((VIS, 1, HALF), F32),
            jax.ShapeDtypeStruct((3, 22, HALF), F32),
            jax.ShapeDtypeStruct((22, HALF), F32),
        ),
        in_specs=[vm] * 3,
        out_specs=[vm] * 3,
    )(gtok, gq, gp)


def per_device(
    tokens, vis_index, owner, enc_gain, enc_qkv, enc_proj, to_decoder, mask_token, dec_gain1,
    dec_qkv, dec_proj, dec_gain2, dec_fc1, dec_fc2, cotangent,
):
    wt = jnp.transpose(enc_qkv, (1, 2, 0)).reshape(3 * HALF, D)
    gtok, gq, gp = run_main(
        tokens[0], vis_index, owner, enc_gain, mask_token, dec_gain1, dec_gain2, wt, enc_proj,
        to_decoder, dec_qkv, dec_proj, dec_fc1, dec_fc2, cotangent[0], jnp.asarray(position_rows()),
    )
    gtok, gq, gp = finish(gtok, gq, gp)
    return jnp.transpose(gtok, (1, 0, 2)), jnp.transpose(gq, (1, 0, 2)), jnp.transpose(gp)


def solution(mesh):
    return jax.shard_map(
        per_device,
        mesh=mesh,
        in_specs=(
            P("dp", None, "fsdp"),
            P("dp", None),
            P("dp", None),
            P(),
            P(None, None, "fsdp"),
            P("fsdp", None),
            P(),
            P(),
            P(),
            P(),
            P(),
            P(),
            P(),
            P(),
            P("dp", "fsdp", None),
        ),
        out_specs=(P("dp", None, "fsdp"), P("dp", None, "fsdp"), P("fsdp", "dp")),
        check_vma=False,
    )
```

```python
import functools
import math

import jax
import jax.numpy as jnp
import numpy as np
from jax import lax
from jax.experimental import pallas as pl
from jax.experimental.pallas import tpu as pltpu
from jax.sharding import PartitionSpec as P

D = 1408
HALF = 704
HD = 88
HEADS = 8
DD = 512
DHD = 64
DH = 4
DI = 256
DF = 2048
TUBES = 1568
VIS = 157
ROWS = 160
OWN = 784
OWNP = 800
QROWS = 160
PADW = 1536
ZB = 384
PA = 384
HP = 176
EPS = 1e-06
ENC_SCALE = HD ** (-0.5)
DEC_SCALE = DHD ** (-0.5)
SQRT_HALF = 0.7071067811865476
INV_SQRT_TWO_PI = 0.3989422804014327
F32 = jnp.float32
BF16 = jnp.bfloat16
MESH = pl.DeviceIdType.MESH
SPREAD_FROM = (0, 256, 640, 1024)
ROUTES = ((2, 1, 0), (1, 0, 2), (0, 2, 1))


def nn(a, b):
    return lax.dot_general(a, b, (((1,), (0,)), ((), ())), preferred_element_type=F32)


def nt(a, b):
    return lax.dot_general(a, b, (((1,), (1,)), ((), ())), preferred_element_type=F32)


def tn(a, b):
    return lax.dot_general(a, b, (((0,), (0,)), ((), ())), preferred_element_type=F32)


def norm_parts(values, width):
    mean = jnp.sum(values, axis=-1, keepdims=True) * (1.0 / width)
    centred = values - mean
    inv = lax.rsqrt(jnp.sum(centred * centred, axis=-1, keepdims=True) * (1.0 / width) + EPS)
    return centred * inv, inv


def norm_back(grad, normed, inv, gain, width):
    scaled = grad * gain
    first = jnp.sum(scaled, axis=-1, keepdims=True) * (1.0 / width)
    second = jnp.sum(scaled * normed, axis=-1, keepdims=True) * (1.0 / width)
    return inv * (scaled - first - normed * second)


def gelu_slope(u):
    return 0.5 * (1.0 + lax.erf(u * SQRT_HALF)) + u * jnp.exp(-0.5 * u * u) * INV_SQRT_TWO_PI


def position_rows():
    rates = np.exp(np.arange(DD // 2, dtype=np.float32) * np.float32(-2.0 * math.log(10000.0) / DD))
    angles = np.arange(TUBES, dtype=np.float32)[:, None] * rates
    return np.stack([np.sin(angles), np.cos(angles)], axis=-1).reshape(TUBES, DD).astype(np.float32)


def main_kernel(
    tok, visr, own, genc, maskt, gain1, gain2,
    wt_h, proj_h, down_h, dqkv_h, dproj_h, fc1_h, fc2_h, cot_h, pos_h,
    gtok, oq, op,
    wt, proj, down, dqkv, dproj, fc1, fc2, cot, pos,
    tokpad, tokrecv, xfull, qs, ks, vs, gms, lows, lowr, rank, rtile, spread,
    xall, kd, vd, kva, xown, qd, qall, mixd, stat, mlp, inv2s, gmid, gmix, gmall,
    exs, exr, hts, htr, sts, strr,
    hid, hidg, mixg, gelp, gelg, rq, gqkv, rqg,
    cs, ra, sa, ta, fa, ga,
    pa, pb, qra, qrb, qsa, qsb, qta, qtb,
    local, send, recv, sh, rh, sm, rm, sg, rg, sq, rqs,
    sx, rx, s3, r3, s4, r4, s5, r5, s6, r6,
):
    me = lax.axis_index("fsdp")
    dp = lax.axis_index("dp")
    z = dp // 16
    y = (dp // 4) % 4
    x = dp % 4
    other = 1 - me
    first = me == 0

    def at_x(i):
        return (z * 16 + y * 4 + i, me)

    def at_y(i):
        return (z * 16 + i * 4 + x, me)

    def at_z(i):
        return (i * 16 + y * 4 + x, me)

    place_on = (at_z, at_y, at_x)
    here = (z, y, x)

    def take(ref, axis, i):
        if axis == 0:
            return ref.at[i]
        return ref.at[:, i] if axis == 1 else ref.at[:, :, i]

    loads = [
        pltpu.make_async_copy(src, dst, local.at[i])
        for i, (src, dst) in enumerate(
            [(wt_h, wt), (proj_h, proj), (down_h, down), (pos_h, pos.at[0:TUBES]), (dqkv_h, dqkv),
             (dproj_h, dproj), (fc1_h, fc1), (fc2_h, fc2), (cot_h, cot.at[0:OWN])]
        )
    ]
    l_wt, l_proj, l_down, l_pos, l_dqkv, l_dproj, l_fc1, l_fc2, l_cot = loads
    l_wt.start()
    l_proj.start()
    l_down.start()

    def push(src, dst, ssem, rsem, place):
        copy = pltpu.make_async_remote_copy(
            src_ref=src, dst_ref=dst, send_sem=ssem, recv_sem=rsem, device_id=place, device_id_type=MESH
        )
        copy.start()
        return copy

    def exchange(src, dst, i):
        return push(src, dst, send.at[i], recv.at[i], (dp, other))

    barrier = pltpu.get_barrier_semaphore()
    pl.semaphore_signal(barrier, inc=1, device_id=(dp, other), device_id_type=MESH)
    for d in range(1, 4):
        for place in (at_x((x + d) % 4), at_y((y + d) % 4), at_z((z + d) % 4)):
            pl.semaphore_signal(barrier, inc=1, device_id=place, device_id_type=MESH)

    cot[OWN:OWNP, :] = jnp.zeros((OWNP - OWN, DD), BF16)
    tokpad[...] = jnp.zeros((ROWS, HALF), BF16)
    tokpad[0:VIS, :] = tok[...]
    pl.semaphore_wait(barrier, 10)
    swap = exchange(tokpad, tokrecv, 0)

    mine_row = (own[...] == me).astype(F32)
    rtile[...] = jnp.zeros((16, 128), F32)
    for i in range(13):
        wide = min(128, TUBES - 128 * i)
        rtile[i:i + 1, 0:wide] = mine_row[:, 128 * i:128 * i + wide]
    tiles = rtile[...]
    upper = lax.broadcasted_iota(jnp.int32, (128, 128), 0) <= lax.broadcasted_iota(jnp.int32, (128, 128), 1)
    inside = nn(tiles.astype(BF16), upper.astype(F32).astype(BF16))
    lower = lax.broadcasted_iota(jnp.int32, (16, 16), 0) > lax.broadcasted_iota(jnp.int32, (16, 16), 1)
    before = nn(lower.astype(F32).astype(BF16), jnp.broadcast_to(inside[:, 127:128], (16, 128)).astype(BF16))
    rtile[...] = jnp.where(tiles > 0.0, inside + before, 0.0)
    for i in range(13):
        wide = min(128, TUBES - 128 * i)
        rank[:, 128 * i:128 * i + wide] = rtile[i:i + 1, 0:wide].astype(jnp.int32) - 1

    lane = lax.broadcasted_iota(jnp.int32, (1, ZB), 1)
    group = (lane.astype(F32) * (1.0 / 24.0) + 0.01).astype(jnp.int32)
    within = lane - group * 24
    for i in range(4):
        shift = 352 * i - SPREAD_FROM[i]
        want = jnp.where(within < 22, group * 22 + within + shift, -1)
        rows = lax.broadcasted_iota(jnp.int32, (512, ZB), 0)
        spread[i] = (rows == want).astype(F32).astype(BF16)

    def spread_cols(v):
        parts = []
        for i in range(4):
            lo = SPREAD_FROM[i]
            hi = min(lo + 512, D)
            parts.append(nn(v[:, lo:hi], spread[i, 0:hi - lo, :]).astype(BF16))
        return parts

    vis_row = visr[...]
    eye = lax.broadcasted_iota(jnp.int32, (ROWS, VIS), 0) == lax.broadcasted_iota(jnp.int32, (ROWS, VIS), 1)
    vis_col = jnp.sum(jnp.where(eye, vis_row + 1, 0), axis=1, keepdims=True) - 1
    vis_hit = lax.broadcasted_iota(jnp.int32, (ROWS, TUBES), 1) == vis_col
    vis_pick = vis_hit.astype(F32).astype(BF16)
    slot_of = jnp.sum(jnp.where(vis_hit, rank[...] + 1, 0), axis=1, keepdims=True) - 1
    own_pick = (lax.broadcasted_iota(jnp.int32, (ROWS, OWNP), 1) == slot_of).astype(F32).astype(BF16)

    swap.wait()
    gain_enc = genc[...].reshape(1, D).astype(F32)

    def all_tokens():
        mine = tokpad[...].astype(F32)
        theirs = tokrecv[...].astype(F32)
        xfull[:, 0:HALF] = jnp.where(first, mine, theirs)
        xfull[:, HALF:D] = jnp.where(first, theirs, mine)
        return xfull[...]

    normed, inv = norm_parts(all_tokens(), D)
    hidden = (normed * gain_enc).astype(BF16)
    for i, part in enumerate(spread_cols(hidden)):
        hid[:, i * ZB:(i + 1) * ZB] = part

    def send_hidden(g):
        axis = ROUTES[g][0]
        return [
            push(hid, hidg.at[g, d - 1], sh.at[g, d - 1], rh.at[g, d - 1], place_on[axis]((here[axis] + d) % 4))
            for d in range(1, 4)
        ]

    hid_sends = [None, None, send_hidden(2)]
    l_wt.wait()
    l_pos.start()
    l_dqkv.start()
    q = (nt(hidden, wt[0:HALF, :]) * ENC_SCALE).astype(BF16)
    k = nt(hidden, wt[HALF:2 * HALF, :]).astype(BF16)
    v = nt(hidden, wt[2 * HALF:3 * HALF, :]).astype(BF16)
    for h in range(HEADS):
        lanes = slice(h * HD, (h + 1) * HD)
        qs[h] = q[:, lanes]
        ks[h] = k[:, lanes]
        vs[h] = v[:, lanes]
    key_ok = lax.broadcasted_iota(jnp.int32, (ROWS, ROWS), 1) < VIS

    def enc_probs(h):
        s = jnp.where(key_ok, nt(qs[h], ks[h]), -1e30)
        e = jnp.exp(s - jnp.max(s, axis=-1, keepdims=True))
        return e * (1.0 / jnp.sum(e, axis=-1, keepdims=True))

    for h in range(HEADS):
        mixg[0, :, h * HD:(h + 1) * HD] = nn(enc_probs(h).astype(BF16), vs[h]).astype(BF16)
    l_proj.wait()
    heads_term = nn(mixg[0], proj[...])
    part_enc = (jnp.where(first, xfull[...], 0.0) + heads_term).astype(BF16)
    l_down.wait()
    lows[...] = nn(part_enc, down[...])
    swap = exchange(lows, lowr, 1)
    l_dproj.start()
    l_fc1.start()
    l_fc2.start()
    l_cot.start()

    swap.wait()
    mix_sends = [
        push(mixg.at[0], mixg.at[d], sm.at[d - 1], rm.at[d - 1], at_z((z + d) % 4)) for d in range(1, 4)
    ]
    hid_sends[0] = send_hidden(0)
    hid_sends[1] = send_hidden(1)
    lowered = (lows[...] + lowr[...]).astype(BF16)
    l_pos.wait()
    l_dqkv.wait()
    gain_one = gain1[...].reshape(1, DD).astype(F32)
    gain_two = gain2[...].reshape(1, DD).astype(F32)
    mask_row = maskt[...].reshape(1, DD).astype(F32)

    vd[...] = jnp.zeros((DH, TUBES, 128), BF16)
    vd[:, :, DHD:DHD + 1] = jnp.ones((DH, TUBES, 1), BF16)

    @pl.loop(0, 2)
    def _(b):
        rows = pl.ds(pl.multiple_of(b * OWN, 16), OWN)
        hit = lax.broadcasted_iota(jnp.int32, (OWN, VIS), 0) + b * OWN == vis_row
        hit = hit.astype(F32)
        placed = nn(hit.astype(BF16), lowered[0:VIS])
        covered = jnp.sum(hit, axis=1, keepdims=True)
        start = (placed + (1.0 - covered) * mask_row + pos[rows, :]).astype(BF16)
        xall[rows, :] = start
        n1, _ = norm_parts(start.astype(F32), DD)
        attn_in = (n1 * gain_one).astype(BF16)
        kv = nn(attn_in, dqkv[:, DI:3 * DI]).astype(BF16)
        kva[rows, :] = kv
        for h in range(DH):
            kd[h, rows, :] = kv[:, h * DHD:(h + 1) * DHD]
            vd[h, rows, 0:DHD] = kv[:, DI + h * DHD:DI + (h + 1) * DHD]

    for lo in (0, 400):
        rows = slice(lo, lo + 400)
        pick = lax.broadcasted_iota(jnp.int32, (400, TUBES), 0) + lo == rank[...]
        start = nn(pick.astype(F32).astype(BF16), xall[...])
        xown[rows, :] = start.astype(BF16)
        n1, _ = norm_parts(start, DD)
        attn_in = (n1 * gain_one).astype(BF16)
        q = (nn(attn_in, dqkv[:, 0:DI]) * DEC_SCALE).astype(BF16)
        qall[rows, :] = q
        for h in range(DH):
            qd[h, rows, :] = q[:, h * DHD:(h + 1) * DHD]

    @pl.loop(0, OWNP // QROWS)
    def _(b):
        rows = pl.ds(pl.multiple_of(b * QROWS, QROWS), QROWS)
        scores = [nt(qd[h, rows, :], kd[h]) for h in range(2)]
        for h in range(DH):
            s = scores[h]
            top = jnp.max(s, axis=-1, keepdims=True)
            if h + 2 < DH:
                scores.append(nt(qd[h + 2, rows, :], kd[h + 2]))
            e = jnp.exp(s - top).astype(BF16)
            o = nn(e, vd[h])
            total = 1.0 / o[:, DHD:DHD + 1]
            stat[rows, h:h + 1] = top
            stat[rows, 4 + h:5 + h] = total
            mixd[rows, h * DHD:(h + 1) * DHD] = o[:, 0:DHD] * total

    l_dproj.wait()

    for lo, hi in ((0, 400), (400, OWNP)):
        after = (xown[lo:hi, :].astype(F32) + nn(mixd[lo:hi, :].astype(BF16), dproj[...])).astype(BF16).astype(F32)
        n2, inv2 = norm_parts(after, DD)
        pos[lo:hi, :] = n2
        inv2s[lo:hi, :] = inv2
        mlp[lo:hi, :] = (n2 * gain_two).astype(BF16)

    l_fc1.wait()
    l_fc2.wait()
    l_cot.wait()
    pos[OWNP:, :] = jnp.zeros((OWNP, DD), F32)

    @pl.loop(0, DF // 512)
    def _(c):
        part = pl.ds(pl.multiple_of(c * 512, 512), 512)
        up = nn(mlp[...], fc1[:, part])
        gact = nt(cot[...], fc2[part, :])
        gup = (gact * gelu_slope(up)).astype(BF16)
        pos[OWNP:, :] += nt(gup, fc1[:, part])

    for lo, hi in ((0, 400), (400, OWNP)):
        g = cot[lo:hi, :].astype(F32) + norm_back(pos[OWNP + lo:OWNP + hi, :], pos[lo:hi, :], inv2s[lo:hi, :], gain_two, DD)
        low = g.astype(BF16)
        gmid[lo:hi, :] = low
        gm = nt(low, dproj[...]).astype(BF16)
        gmall[lo:hi, :] = gm
        prod = gm.astype(F32) * mixd[lo:hi, :]
        for h in range(DH):
            lanes = slice(h * DHD, (h + 1) * DHD)
            gmix[h, lo:hi, :] = gm[:, lanes]
            stat[lo:hi, 8 + h:9 + h] = jnp.sum(prod[:, lanes], axis=-1, keepdims=True)

    vis_x = nn(vis_pick, xall[...])
    vis_kv = nn(vis_pick, kva[...]).astype(BF16)
    vis_q = nn(own_pick, qall[...]).astype(BF16)
    vis_g = nn(own_pick, gmall[...]).astype(BF16)
    exs[:, 3 * DI:] = nn(own_pick, gmid[...]).astype(BF16)
    for h in range(DH):
        lanes = slice(h * DHD, (h + 1) * DHD)
        k_vis = vis_kv[:, lanes]
        v_vis = vis_kv[:, DI + h * DHD:DI + (h + 1) * DHD]
        p = jnp.exp(nt(qd[h], k_vis) - stat[:, h:h + 1]) * stat[:, 4 + h:5 + h]
        ds = (p * (nt(gmix[h], v_vis) - stat[:, 8 + h:9 + h])).astype(BF16)
        exs[:, DI + h * DHD:DI + (h + 1) * DHD] = tn(ds, qd[h]).astype(BF16)
        exs[:, 2 * DI + h * DHD:2 * DI + (h + 1) * DHD] = tn(p.astype(BF16), gmix[h]).astype(BF16)
        s = nt(vis_q[:, lanes], kd[h])
        e = jnp.exp(s - jnp.max(s, axis=-1, keepdims=True))
        p = e * (1.0 / jnp.sum(e, axis=-1, keepdims=True))
        g = nt(vis_g[:, lanes], vd[h, :, 0:DHD])
        c = jnp.sum(p * g, axis=-1, keepdims=True)
        ds = (p * (g - c)).astype(BF16)
        exs[:, lanes] = (nn(ds, kd[h]) * DEC_SCALE).astype(BF16)

    swap = exchange(exs, exr, 2)
    swap.wait()
    both = exs[...].astype(F32) + exr[...].astype(F32)
    gattn = nt(both[:, 0:3 * DI].astype(BF16), dqkv[...])
    n1, inv1 = norm_parts(vis_x, DD)
    gstart = both[:, 3 * DI:] + norm_back(gattn, n1, inv1, gain_one, DD)
    real = lax.broadcasted_iota(jnp.int32, (ROWS, DD), 0) < VIS
    glow = jnp.where(real, gstart, 0.0).astype(BF16)

    genc_rows = nt(glow, down[...])
    gel = genc_rows.astype(BF16)
    for i, part in enumerate(spread_cols(gel)):
        gelp[i] = part
    gel_sends = []
    for d in range(1, 4):
        zi = (z + d) % 4
        gel_sends.append(push(gelp.at[zi], gelg.at[d], sg.at[d - 1], rg.at[d - 1], at_z(zi)))
    gelg[0] = gelp[z]
    gmx = nt(gel, proj[...]).astype(BF16)
    for h in range(HEADS):
        gms[h] = gmx[:, h * HD:(h + 1) * HD]
    for h in range(HEADS):
        p = enc_probs(h)
        gm = gms[h]
        g = nt(gm, vs[h])
        c = jnp.sum(p * g, axis=-1, keepdims=True)
        ds = (p * (g - c)).astype(BF16)
        three = ((nn(ds, ks[h]) * ENC_SCALE).astype(BF16), tn(ds, qs[h]).astype(BF16), tn(p.astype(BF16), gm).astype(BF16))
        lanes = slice((h % 2) * HD, (h % 2 + 1) * HD)
        for part in range(3):
            rq[part, h // 2, :, lanes] = three[part]
            gqkv[:, part * HALF + h * HD:part * HALF + (h + 1) * HD] = three[part]
    rq_sends = []
    for g in range(3):
        axis = ROUTES[g][0]
        sends = []
        for d in range(1, 4):
            i = (here[axis] + d) % 4
            sends.append(push(rq.at[g, i], rqg.at[g, d - 1], sq.at[g, d - 1], rqs.at[g, d - 1], place_on[axis](i)))
        rq_sends.append(sends)

    def total(mine, got):
        return (mine.astype(F32) + got[0].astype(F32)) + (got[1].astype(F32) + got[2].astype(F32))

    for copy in gel_sends:
        copy.wait()
    for copy in mix_sends:
        copy.wait()
    prod = tn(gelg[...].reshape(4 * ROWS, ZB), mixg[...].reshape(4 * ROWS, HALF)).astype(BF16).reshape(4, 4, 24, HALF)
    pa[...] = prod[:, :, :, 0:PA].reshape(4, 96, PA)
    for i in range(4):
        pb[i, :, :, 0:HALF - PA] = prod[:, i, :, PA:HALF]
        pb[i, :, :, HALF - PA:PA] = jnp.zeros((4, 24, 2 * PA - HALF), BF16)
    p_sends = []
    for d in range(1, 4):
        yi = (y + d) % 4
        xi = (x + d) % 4
        p_sends.append(push(pa.at[yi], qra.at[d - 1], s5.at[0, d - 1], r5.at[0, d - 1], at_y(yi)))
        p_sends.append(push(pb.at[xi], qrb.at[d - 1], s5.at[1, d - 1], r5.at[1, d - 1], at_x(xi)))

    terms = nn(gqkv[...], wt[...]).astype(BF16)
    scaled = terms.astype(F32) * gain_enc
    normed, inv = norm_parts(all_tokens(), D)
    s1 = jnp.sum(scaled, axis=-1, keepdims=True)
    s2 = jnp.sum(scaled * normed, axis=-1, keepdims=True)
    sts[...] = jnp.where(lax.broadcasted_iota(jnp.int32, (ROWS, 128), 1) == 0, s1, s2)
    hts[...] = jnp.where(first, terms[:, HALF:], terms[:, 0:HALF])
    swap_a = exchange(hts, htr, 3)
    swap_b = exchange(sts, strr, 4)

    second = []
    for g in range(3):
        gather, one, _ = ROUTES[g]
        for copy in hid_sends[g] + rq_sends[g]:
            copy.wait()
        prod = tn(hidg[g].reshape(3 * ROWS, PADW), rqg[g].reshape(3 * ROWS, HP)) + tn(hid[...], rq[g, here[gather]])
        cs[g] = prod.reshape(4, 4, 4, 24, HP).astype(BF16)
        for d in range(1, 4):
            i = (here[one] + d) % 4
            second.append(push(take(cs.at[g], one, i), ra.at[g, d - 1], sx.at[g, d - 1], rx.at[g, d - 1], place_on[one](i)))

    swap_a.wait()
    swap_b.wait()
    stats = sts[...] + strr[...]
    m1 = stats[:, 0:1] * (1.0 / D)
    m2 = stats[:, 1:2] * (1.0 / D)
    gh = jnp.where(first, terms[:, 0:HALF], terms[:, HALF:]).astype(F32) + htr[...].astype(F32)
    gain_mine = jnp.where(first, gain_enc[:, 0:HALF], gain_enc[:, HALF:])
    normed_mine = jnp.where(first, normed[:, 0:HALF], normed[:, HALF:])
    base = jnp.where(first, genc_rows[:, 0:HALF], genc_rows[:, HALF:D])
    out = base + inv * (gh * gain_mine - m1 - normed_mine * m2)
    gtok[...] = out[0:VIS, :]

    for copy in p_sends:
        copy.wait()
    qsa[...] = total(pa[y], qra).astype(BF16).reshape(4, 24, PA)
    qsb[...] = total(pb[x], qrb).astype(BF16)
    p_sends = []
    for d in range(1, 4):
        yi = (y + d) % 4
        xi = (x + d) % 4
        p_sends.append(push(qsa.at[xi], qta.at[d - 1], s6.at[0, d - 1], r6.at[0, d - 1], at_x(xi)))
        p_sends.append(push(qsb.at[yi], qtb.at[d - 1], s6.at[1, d - 1], r6.at[1, d - 1], at_y(yi)))

    third = []
    for g in range(3):
        gather, one, two = ROUTES[g]
        for copy in second[3 * g:3 * g + 3]:
            copy.wait()
        sa[g] = total(take(cs.at[g], one, here[one])[...], ra.at[g]).astype(BF16)
        rest = [axis for axis in range(3) if axis != one].index(two)
        for d in range(1, 4):
            i = (here[two] + d) % 4
            third.append(push(take(sa.at[g], rest, i), ta.at[g, d - 1], s3.at[g, d - 1], r3.at[g, d - 1], place_on[two](i)))
    for copy in p_sends:
        copy.wait()
    op[:, 0:PA] = total(qsa[x], qta)[0:22, :]
    op[:, PA:HALF] = total(qsb[y], qtb)[0:22, 0:HALF - PA]
    fourth = []
    for g in range(3):
        gather, one, two = ROUTES[g]
        for copy in third[3 * g:3 * g + 3]:
            copy.wait()
        rest = [axis for axis in range(3) if axis != one].index(two)
        fa[g] = total(take(sa.at[g], rest, here[two])[...], ta.at[g])
        for d in range(1, 4):
            i = (here[gather] + d) % 4
            fourth.append(push(fa.at[g, i], ga.at[g, here[gather]], s4.at[g, d - 1], r4.at[g, d - 1], place_on[gather](i)))
        ga[g, here[gather]] = fa[g, here[gather]]
    for copy in fourth:
        copy.wait()
    for g in range(3):
        for i in range(4):
            oq[g, :, HP * i:HP * (i + 1)] = ga[g, i][0:22, :]


def run_main(tok, visr, own, genc, maskt, gain1, gain2, wt, proj, down, dqkv, dproj, fc1, fc2, cot, pos):
    vm = pl.BlockSpec(memory_space=pltpu.VMEM)
    hbm = pl.BlockSpec(memory_space=pl.ANY)
    V = pltpu.VMEM
    S = pltpu.SemaphoreType.DMA
    big = (wt, proj, down, dqkv, dproj, fc1, fc2, cot, pos)
    half = (ROWS, HALF)
    scratch = [V(a.shape, a.dtype) for a in big[:7]] + [
        V((OWNP, DD), BF16), V((2 * OWNP, DD), F32),
        V(half, BF16), V(half, BF16), V((ROWS, D), F32),
        V((HEADS, ROWS, HD), BF16), V((HEADS, ROWS, HD), BF16), V((HEADS, ROWS, HD), BF16),
        V((HEADS, ROWS, HD), BF16),
        V((ROWS, DD), F32), V((ROWS, DD), F32), V((1, TUBES), jnp.int32), V((16, 128), F32), V((4, 512, ZB), BF16),
        V((TUBES, DD), BF16), V((DH, TUBES, DHD), BF16), V((DH, TUBES, 128), BF16), V((TUBES, 2 * DI), BF16),
        V((OWNP, DD), BF16), V((DH, OWNP, DHD), BF16), V((OWNP, DI), BF16), V((OWNP, DI), F32),
        V((OWNP, 16), F32),
        V((OWNP, DD), BF16), V((OWNP, 1), F32), V((OWNP, DD), BF16),
        V((DH, OWNP, DHD), BF16), V((OWNP, DI), BF16),
        V((ROWS, 3 * DI + DD), BF16), V((ROWS, 3 * DI + DD), BF16),
        V(half, BF16), V(half, BF16), V((ROWS, 128), F32), V((ROWS, 128), F32),
        V((ROWS, PADW), BF16), V((3, 3, ROWS, PADW), BF16),
        V((4, ROWS, HALF), BF16), V((4, ROWS, ZB), BF16), V((4, ROWS, ZB), BF16),
        V((3, 4, ROWS, HP), BF16), V((ROWS, 3 * HALF), BF16), V((3, 3, ROWS, HP), BF16),
        V((3, 4, 4, 4, 24, HP), BF16), V((3, 3, 4, 4, 24, HP), BF16),
        V((3, 4, 4, 24, HP), BF16), V((3, 3, 4, 24, HP), BF16), V((3, 4, 24, HP), F32), V((3, 4, 24, HP), F32),
        V((4, 96, PA), BF16), V((4, 4, 24, PA), BF16), V((3, 96, PA), BF16), V((3, 4, 24, PA), BF16),
        V((4, 24, PA), BF16), V((4, 24, PA), BF16), V((3, 24, PA), BF16), V((3, 24, PA), BF16),
        S((9,)), S((5,)), S((5,)), S((3, 3)), S((3, 3)), S((3,)), S((3,)), S((3,)), S((3,)), S((3, 3)), S((3, 3)),
        S((3, 3)), S((3, 3)), S((3, 3)), S((3, 3)), S((3, 3)), S((3, 3)),
        S((2, 3)), S((2, 3)), S((2, 3)), S((2, 3)),
    ]
    return pl.pallas_call(
        main_kernel,
        out_shape=(
            jax.ShapeDtypeStruct((VIS, HALF), F32),
            jax.ShapeDtypeStruct((3, 22, HALF), F32),
            jax.ShapeDtypeStruct((22, HALF), F32),
        ),
        in_specs=[vm] * 7 + [hbm] * 9,
        out_specs=[vm] * 3,
        scratch_shapes=scratch,
        compiler_params=pltpu.CompilerParams(
            collective_id=0, has_side_effects=True, vmem_limit_bytes=60 * 1024 * 1024
        ),
    )(tok, visr, own, genc, maskt, gain1, gain2, *big)


def finish_kernel(gtok, gq, gp, tok_o, q_o, p_o):
    tok_o[...] = gtok[...].reshape(VIS, 1, HALF)
    q_o[...] = gq[...]
    p_o[...] = gp[...]


def finish(gtok, gq, gp):
    vm = pl.BlockSpec(memory_space=pltpu.VMEM)
    return pl.pallas_call(
        finish_kernel,
        out_shape=(
            jax.ShapeDtypeStruct((VIS, 1, HALF), F32),
            jax.ShapeDtypeStruct((3, 22, HALF), F32),
            jax.ShapeDtypeStruct((22, HALF), F32),
        ),
        in_specs=[vm] * 3,
        out_specs=[vm] * 3,
    )(gtok, gq, gp)


def per_device(
    tokens, vis_index, owner, enc_gain, enc_qkv, enc_proj, to_decoder, mask_token, dec_gain1,
    dec_qkv, dec_proj, dec_gain2, dec_fc1, dec_fc2, cotangent,
):
    wt = jnp.transpose(enc_qkv, (1, 2, 0)).reshape(3 * HALF, D)
    gtok, gq, gp = run_main(
        tokens[0], vis_index, owner, enc_gain, mask_token, dec_gain1, dec_gain2, wt, enc_proj,
        to_decoder, dec_qkv, dec_proj, dec_fc1, dec_fc2, cotangent[0], jnp.asarray(position_rows()),
    )
    gtok, gq, gp = finish(gtok, gq, gp)
    return jnp.transpose(gtok, (1, 0, 2)), jnp.transpose(gq, (1, 0, 2)), jnp.transpose(gp)


def solution(mesh):
    return jax.shard_map(
        per_device,
        mesh=mesh,
        in_specs=(
            P("dp", None, "fsdp"),
            P("dp", None),
            P("dp", None),
            P(),
            P(None, None, "fsdp"),
            P("fsdp", None),
            P(),
            P(),
            P(),
            P(),
            P(),
            P(),
            P(),
            P(),
            P("dp", "fsdp", None),
        ),
        out_specs=(P("dp", None, "fsdp"), P("dp", None, "fsdp"), P("fsdp", "dp")),
        check_vma=False,
    )
```
